256 devices in a mesh: ctx: 64 (over z, x, core), head: 4 (over y).
Axes of the slice: x: 4, y: 4, z: 8, core: 2. Of those that a mesh axis runs over, the one named last changes fastest.
Arguments:
- out_grad: bfloat16 [32768, 2560], P('ctx', 'head'), may hold values from -0.3125 to 0.3125
- out_proj: bfloat16 [2048, 2560], P('head'), may hold values from -0.125 to 0.125
- query_rows: bfloat16 [32768, 2048], P('ctx', 'head'), may hold values from -6 to 6
- key_rows: bfloat16 [32768, 2048], P('ctx', 'head'), may hold values from -6 to 6
- value_rows: bfloat16 [32768, 2048], P('ctx', 'head'), may hold values from -6 to 6
- log_decay: float32 [8, 32768], P('head', 'ctx'), as said below
- doc_starts: int32 [3], replicated, may hold values from 1 to 32767, as said below
Outputs:
- query_grad: float32 [32768, 2048], P('ctx', 'head')
- key_grad: float32 [32768, 2048], P('ctx', 'head')
- value_grad: float32 [32768, 2048], P('ctx', 'head')
The draws below stay inside these ranges and needn't reach their ends.
Inputs may be any that keep to these rules, and one draw needn't show every extreme that they name: `doc_starts`: 3 strictly increasing token positions, each at least 1 and below 32768. `log_decay`: every entry is negative; each head's decays vary from token to token.
All inputs are finite; a program needn't handle non-finite values.
Results may differ from the reference program's by a relative error of at most 0.0049.
Values may be sent and summed in bfloat16 or wider, within the bound.
A program may use at most 192 MiB of HBM per device.

```python
import jax
import jax.numpy as jnp
from jax import lax

D = 2560
HEAD_SIZE = 256
ATTENTION_LANES = 8
HV = 2048
TOK_DEV = 512
SEQUENCE_SPAN = 32768
DOCS = 3


def draw_log_decay(key, part):
    key = jax.random.fold_in(key, 11)
    keys = jax.random.split(key, 8)
    fast_count = ATTENTION_LANES // 2
    ranks = jax.random.permutation(keys[0], ATTENTION_LANES)
    fast_rate = jnp.exp(jax.random.uniform(keys[1], (ATTENTION_LANES,), jnp.float32, jnp.log(0.1), jnp.log(0.6))) / TOK_DEV
    quick_rate = jnp.exp(jax.random.uniform(keys[2], (ATTENTION_LANES,), jnp.float32, jnp.log(1.0 / 50.0), jnp.log(1.0 / 32.0)))
    fast_rate = jnp.where(ranks == 0, quick_rate, fast_rate)
    slow_rate = jnp.exp(jax.random.uniform(keys[3], (ATTENTION_LANES,), jnp.float32, jnp.log(0.15), jnp.log(0.3))) / SEQUENCE_SPAN
    forgetting_speed = jnp.where(ranks < fast_count, fast_rate, slow_rate)[:, None]
    segment_scaling = jnp.exp(jax.random.uniform(keys[4], (ATTENTION_LANES, SEQUENCE_SPAN // TOK_DEV), jnp.float32, jnp.log(0.5), jnp.log(2.0)))
    segment_scaling = jnp.repeat(segment_scaling, TOK_DEV, axis=1)
    approximate_guess = jnp.exp(jax.random.uniform(keys[5], (ATTENTION_LANES, SEQUENCE_SPAN), jnp.float32, jnp.log(0.4), jnp.log(2.5)))
    places = jax.random.randint(keys[6], (ATTENTION_LANES, 6), 0, SEQUENCE_SPAN)
    objective_terms = jnp.log(jax.random.uniform(keys[7], (ATTENTION_LANES, 6), jnp.float32, 0.75, 0.8))
    positions = jnp.arange(SEQUENCE_SPAN, dtype=jnp.int32)[None, :]
    clustered_spans = jnp.zeros((ATTENTION_LANES, SEQUENCE_SPAN), jnp.float32)
    for selected_option in range(6):
        masked_positions = (positions == places[:, selected_option:selected_option + 1]).astype(jnp.float32)
        clustered_spans = clustered_spans + objective_terms[:, selected_option:selected_option + 1] * masked_positions
    return (-forgetting_speed * segment_scaling * approximate_guess + clustered_spans).astype(jnp.float32)


def draw_doc_starts(key, part):
    key = jax.random.fold_in(key, 23)
    chosen = jax.random.permutation(key, SEQUENCE_SPAN - 2)[:DOCS - 2] + 2
    ends = jnp.array([1, SEQUENCE_SPAN - 1], dtype=jnp.int32)
    return jnp.sort(jnp.concatenate([chosen.astype(jnp.int32), ends]))


def shard_levels(stream_key, shape, pieces, low, largest):
    loudness = 1.0
    for position, shards_of in pieces:
        draws = jax.random.uniform(jax.random.fold_in(jax.random.fold_in(stream_key, 6), position), (shards_of,), jnp.float32, low / len(pieces), largest / len(pieces))
        loudness = loudness * jnp.repeat(jnp.exp(draws), shape[position] // shards_of).reshape((-1,) + (1,) * (len(shape) - 1 - position))
    return loudness


def noise(key, shape, scale, bound, cuts=(), held_as=jnp.bfloat16):
    drawn = jax.random.normal(key, shape, jnp.float32) * scale
    if len(cuts) > 0:
        drawn = shard_levels(key, shape, cuts, -0.22, 0.18) * drawn
    return jnp.clip(drawn, min=-bound, max=bound).astype(held_as)


def setup_inputs(seed: int = 0) -> dict:
    splits = jax.random.split(jax.random.key(seed), 8)
    return {
        "out_grad": noise(splits[0], (SEQUENCE_SPAN, D), (4 * SEQUENCE_SPAN ** -0.5), 0.3125, ((0, 64), (1, 4))),
        "out_proj": noise(splits[1], (HV, D), D ** -0.5, 0.125, ((0, 4),)),
        "query_rows": noise(splits[2], (SEQUENCE_SPAN, HV), 1.0, 6.0, ((0, 64), (1, 4))),
        "key_rows": noise(splits[3], (SEQUENCE_SPAN, HV), 1.0, 6.0, ((0, 64), (1, 4))),
        "value_rows": noise(splits[4], (SEQUENCE_SPAN, HV), 1.0, 6.0, ((0, 64), (1, 4))),
        "log_decay": draw_log_decay(jax.random.fold_in(splits[7], 71), 0),
        "doc_starts": draw_doc_starts(jax.random.fold_in(splits[7], 71), 0),
    }


HIGH = lax.Precision.HIGHEST


def rounded(value):
    return lax.optimization_barrier(value.astype(jnp.bfloat16)).astype(jnp.float32)


def geometry(log_block, doc_starts, offset):
    length = log_block.shape[1]
    places = offset + jnp.arange(length, dtype=jnp.int32)
    segment = jnp.sum((doc_starts[None, :] <= places[:, None]).astype(jnp.int32), axis=1)
    before = jnp.sum((doc_starts <= offset - 1).astype(jnp.int32))
    cumulative = jnp.cumsum(log_block, axis=1)
    inflow = jnp.exp(cumulative) * (segment == before).astype(jnp.float32)[None, :]
    outflow = jnp.exp(cumulative[:, -1:] - cumulative) * (segment == segment[-1]).astype(jnp.float32)[None, :]
    return cumulative, segment, inflow, outflow


def pair_weights(cumulative, segment):
    length = segment.shape[0]
    order = jnp.arange(length, dtype=jnp.int32)
    causal = (segment[:, None] == segment[None, :]) & (order[None, :] <= order[:, None])
    spread = cumulative[:, :, None] - cumulative[:, None, :]
    return jnp.exp(jnp.where(causal[None], spread, -1e30))


def combine(earlier, later):
    return (earlier[0] * later[0], later[0][:, None, None] * earlier[1] + later[1])


def reference(out_grad, out_proj, query_rows, key_rows, value_rows, log_decay, doc_starts):
    factor = HEAD_SIZE ** -0.5
    grad_all = jnp.dot(out_grad, out_proj.T, preferred_element_type=jnp.float32).astype(jnp.bfloat16)
    scaled_all = query_rows * factor
    blocks = SEQUENCE_SPAN // TOK_DEV
    shaped = (blocks, TOK_DEV, ATTENTION_LANES, HEAD_SIZE)
    grads = grad_all.reshape(shaped)
    queries = scaled_all.reshape(shaped)
    keysets = key_rows.reshape(shaped)
    valuesets = value_rows.reshape(shaped)
    log_blocks = log_decay.reshape(ATTENTION_LANES, blocks, TOK_DEV).transpose(1, 0, 2)
    indices = jnp.arange(blocks, dtype=jnp.int32)

    def summary_of(index):
        cumulative, segment, inflow, outflow = geometry(log_blocks[index], doc_starts, index * TOK_DEV)
        decayed_keys = rounded(keysets[index].astype(jnp.float32) * outflow.T[:, :, None])
        decayed_queries = rounded(queries[index].astype(jnp.float32) * inflow.T[:, :, None])
        forward_state = jnp.einsum('thd,the->hde', decayed_keys, valuesets[index].astype(jnp.float32), precision=HIGH)
        adjoint_state = jnp.einsum('thd,the->hde', decayed_queries, grads[index].astype(jnp.float32), precision=HIGH)
        return inflow[:, -1], forward_state, adjoint_state

    totals, forward_states, adjoint_states = lax.map(summary_of, indices)
    identity = (jnp.ones((ATTENTION_LANES,), jnp.float32), jnp.zeros((ATTENTION_LANES, HEAD_SIZE, HEAD_SIZE), jnp.float32))

    def advance(running, item):
        return combine(running, item), running[1]

    _, states_in = lax.scan(advance, identity, (totals, forward_states))
    _, adjoints_in = lax.scan(advance, identity, (totals, adjoint_states), reverse=True)

    def outputs_of(item):
        index, state_in, adjoint_in = item
        state_in = rounded(state_in)
        adjoint_in = rounded(adjoint_in)
        cumulative, segment, inflow, outflow = geometry(log_blocks[index], doc_starts, index * TOK_DEV)
        weights = pair_weights(cumulative, segment)
        grad_here = grads[index].astype(jnp.float32)
        query_here = queries[index].astype(jnp.float32)
        key_here = keysets[index].astype(jnp.float32)
        value_here = valuesets[index].astype(jnp.float32)
        first_mixed = rounded(jnp.einsum('thd,shd->hts', grad_here, value_here, precision=HIGH) * weights)
        second_mixed = rounded(jnp.einsum('thd,shd->hts', query_here, key_here, precision=HIGH) * weights)
        query_grad = factor * (jnp.einsum('hts,shd->thd', first_mixed, key_here, precision=HIGH) + inflow.T[:, :, None] * jnp.einsum('the,hde->thd', grad_here, state_in, precision=HIGH))
        key_grad = jnp.einsum('hts,thd->shd', first_mixed, query_here, precision=HIGH) + outflow.T[:, :, None] * jnp.einsum('she,hde->shd', value_here, adjoint_in, precision=HIGH)
        value_grad = jnp.einsum('hts,the->she', second_mixed, grad_here, precision=HIGH) + outflow.T[:, :, None] * jnp.einsum('shd,hde->she', key_here, adjoint_in, precision=HIGH)
        return query_grad, key_grad, value_grad

    query_grad, key_grad, value_grad = lax.map(outputs_of, (indices, states_in, adjoints_in))
    return (query_grad.reshape(SEQUENCE_SPAN, HV), key_grad.reshape(SEQUENCE_SPAN, HV), value_grad.reshape(SEQUENCE_SPAN, HV))
```

```python
import functools

import jax
import jax.numpy as jnp
from jax import lax
from jax.experimental import pallas as pl
from jax.experimental.pallas import tpu as pltpu
from jax.sharding import PartitionSpec as P

PLANE = 8
CHUNKS = 4
MESH = pl.DeviceIdType.MESH
F32 = jnp.float32
BF16 = jnp.bfloat16


def nn(a, b):
    return lax.dot_general(a, b, (((1,), (0,)), ((), ())), preferred_element_type=F32)


def nt(a, b):
    return lax.dot_general(a, b, (((1,), (1,)), ((), ())), preferred_element_type=F32)


def tn(a, b):
    return lax.dot_general(a, b, (((0,), (0,)), ((), ())), preferred_element_type=F32)


def kernel(
    planes, members,
    doc, ld, og, w, q, k, v,
    qg, kg, vg,
    og_v, w_v, q_v, k_v, v_v, acc, g_v, wt, sm, fm, dq, inc, outc, qg_v, kg_v, vg_v,
    t_send, t_rec, s_send, s_rec, pre, zf_send, zf_rec, za_send, za_rec, zb_send, zb_rec,
    o_send, st_in,
    local_sem, out_sem, y_send, y_rec, t_sem, c_send, c_rec,
):
    tokens, width = q_v.shape
    feats = og_v.shape[2]
    size = width // 2
    rows = s_send.shape[2]
    sub = za_send.shape[1]
    chunk = tokens // CHUNKS
    factor = size ** -0.5
    ctx, y = lax.axis_index("ctx"), lax.axis_index("head")
    z, p = ctx // members, ctx % members
    right, left = (y + 1) % 4, (y + 3) % 4
    owners = (y, left, right, (y + 2) % 4)

    loads = [pltpu.make_async_copy(og, og_v.at[0], local_sem.at[0])]
    for i, (src, dst) in enumerate(((k, k_v), (v, v_v), (q, q_v))):
        loads.append(pltpu.make_async_copy(src, dst, local_sem.at[1 + i]))
    for i in range(4):
        start = pl.multiple_of(owners[i] * feats, 128)
        loads.append(pltpu.make_async_copy(w.at[:, pl.ds(start, feats)], w_v.at[i], local_sem.at[4 + i]))
    for load in loads:
        load.start()

    barrier = pltpu.get_barrier_semaphore()
    for other in (left, right):
        pl.semaphore_signal(barrier, inc=1, device_id=(ctx, other), device_id_type=MESH)

    def greet_plane(d, c):
        pl.semaphore_signal(barrier, inc=1, device_id=(z * members + (p + d) % members, y), device_id_type=MESH)
        return c

    def greet_z(d, c):
        pl.semaphore_signal(barrier, inc=1, device_id=(((z + d) % planes) * members + p, y), device_id_type=MESH)
        return c

    lax.fori_loop(1, members, greet_plane, 0)
    lax.fori_loop(1, planes, greet_z, 0)
    pl.semaphore_wait(barrier, 2 + (members - 1) + (planes - 1))

    def hop(src_slot, dst_slot, c, to, lane):
        at = pl.ds(c * chunk, chunk)
        return pltpu.make_async_remote_copy(
            src_ref=og_v.at[src_slot, at], dst_ref=og_v.at[dst_slot, at],
            send_sem=y_send.at[lane, c], recv_sem=y_rec.at[dst_slot - 1, c],
            device_id=(ctx, to), device_id_type=MESH,
        )

    to_right = [hop(0, 1, c, right, 0) for c in range(CHUNKS)]
    to_left = [hop(0, 2, c, left, 1) for c in range(CHUNKS)]
    onward = [hop(1, 3, c, right, 2) if c < CHUNKS // 2 else hop(2, 3, c, left, 2) for c in range(CHUNKS)]
    loads[0].wait()
    for c in range(CHUNKS):
        to_right[c].start()
        to_left[CHUNKS - 1 - c].start()

    offset = ctx * tokens
    lane = lax.broadcasted_iota(jnp.int32, (8, tokens), 1)
    docs = [doc[i] for i in range(doc.shape[0])]

    def segment(places):
        total = jnp.zeros(places.shape, jnp.int32)
        for d in docs:
            total = total + (d <= places).astype(jnp.int32)
        return total

    def segment_at(place):
        total = jnp.int32(0)
        for d in docs:
            total = total + (d <= place).astype(jnp.int32)
        return total

    before, last = segment_at(offset - 1), segment_at(offset + tokens - 1)
    seg_row = segment(offset + lane)[0:1]
    row_at = lax.broadcasted_iota(jnp.int32, (tokens, tokens), 0)
    col_at = lax.broadcasted_iota(jnp.int32, (tokens, tokens), 1)
    seg_col = segment(offset + lax.broadcasted_iota(jnp.int32, (tokens, 1), 0))
    in_row = (seg_row == before).astype(F32)
    in_col = (seg_col == before).astype(F32)
    out_col = (seg_col == last).astype(F32)
    same = (seg_col == seg_row) & (col_at <= row_at)
    cums = []
    for h in range(2):
        cum = jnp.broadcast_to(ld[h : h + 1, :], (8, tokens))
        step = 1
        while step < tokens:
            cum = cum + jnp.where(lane >= step, pltpu.roll(cum, step, 1), 0.0)
            step *= 2
        whole = jnp.sum(jnp.where(lane == tokens - 1, cum, 0.0), axis=1, keepdims=True)
        through = jnp.exp(whole) * jnp.where(before == last, 1.0, 0.0)
        t_send[h] = jnp.broadcast_to(through, (8, t_send.shape[2]))
        cum_row = cum[0:1]
        cum_col = jnp.sum(jnp.where(row_at == col_at, cum_row, 0.0), axis=1, keepdims=True)
        inc[h] = jnp.exp(cum_col) * in_col
        outc[h] = jnp.exp(whole[0:1] - cum_col) * out_col
        cums.append((cum_row, cum_col))

    def plane_copy(j, src, dst, send, recv):
        return pltpu.make_async_remote_copy(
            src_ref=src, dst_ref=dst, send_sem=send, recv_sem=recv,
            device_id=(z * members + j, y), device_id_type=MESH,
        )

    def z_copy(j, src, dst, send, recv):
        return pltpu.make_async_remote_copy(
            src_ref=src, dst_ref=dst, send_sem=send, recv_sem=recv,
            device_id=(j * members + p, y), device_id_type=MESH,
        )

    def send_plane(src, dst, send, recv, index=lambda j: j):
        def one(d, c):
            j = (p + d) % members
            plane_copy(j, src.at[index(j)], dst.at[p], send, recv).start()
            return c

        lax.fori_loop(1, members, one, 0)

    def send_z(src, dst, send, recv):
        def one(d, c):
            j = (z + d) % planes
            z_copy(j, src.at[j], dst.at[z], send, recv).start()
            return c

        lax.fori_loop(1, planes, one, 0)

    def arrived(ref, count, sem):
        part = ref.at[pl.ds(0, count)]
        pltpu.make_async_copy(part, part, sem).wait()

    heads_per = members // 2
    send_plane(t_send, t_rec, t_sem.at[0], t_sem.at[1], lambda j: j // heads_per)
    t_rec[p] = t_send[p // heads_per]

    def first(direction, h, state):
        s_send[direction, pl.ds(h * heads_per, heads_per)] = state.astype(BF16).reshape(heads_per, rows, size)

    def first_send(direction):
        send_plane(s_send.at[direction], s_rec.at[direction], c_send.at[direction, 0], c_rec.at[direction, 0])
        s_rec[direction, p] = s_send[direction, p]

    def second_send(direction):
        arrived(s_rec.at[direction], members - 1, c_rec.at[direction, 0])
        run = jnp.zeros((rows, size), F32)
        decay = jnp.ones((1, 1), F32)
        order = range(members) if direction == 0 else reversed(range(members))
        for i in order:
            pre[direction, i] = run
            t = t_rec[i, 0:1, 0:1]
            run = t * run + s_rec[direction, i].astype(F32)
            decay = decay * t
        parts = run.reshape(planes, sub, size)
        if direction == 0:
            zf_send[:, 0:sub] = parts
            zf_send[:, sub:] = jnp.broadcast_to(decay.reshape(1, 1, 1), (planes, 8, size))
            send, rec = zf_send, zf_rec
        else:
            za_send[...] = parts
            send, rec = za_send, za_rec
        send_z(send, rec, c_send.at[direction, 1], c_rec.at[direction, 1])
        rec[z] = send[z]

    def third_send(direction):
        rec = za_rec if direction else zf_rec
        arrived(rec, planes - 1, c_rec.at[direction, 1])
        run = jnp.zeros((sub, size), F32)
        order = range(planes) if direction == 0 else reversed(range(planes))
        for i in order:
            zb_send[direction, i] = run
            run = zf_rec[i, sub : sub + 1] * run + rec[i, 0:sub]
        send_z(zb_send.at[direction], zb_rec.at[direction], c_send.at[direction, 2], c_rec.at[direction, 2])
        zb_rec[direction, z] = zb_send[direction, z]

    def fourth_send(direction):
        arrived(zb_rec.at[direction], planes - 1, c_rec.at[direction, 2])
        entering = zb_rec[direction].reshape(rows, size)
        decay = jnp.ones((1, 1), F32)
        order = range(members) if direction == 0 else reversed(range(members))
        for i in order:
            o_send[direction, i] = (pre[direction, i] + decay * entering).astype(BF16)
            decay = decay * t_rec[i, 0:1, 0:1]
        send_plane(o_send.at[direction], st_in.at[direction], c_send.at[direction, 3], c_rec.at[direction, 3])
        st_in[direction, p] = o_send[direction, p]

    def state(direction, h):
        arr = st_in[direction, pl.ds(h * heads_per, heads_per)]
        return arr.reshape(size, size)

    def cols(h):
        return slice(h * size, (h + 1) * size)

    loads[1].wait()
    loads[2].wait()
    for h in range(2):
        decayed = (k_v[:, cols(h)].astype(F32) * outc[h]).astype(BF16)
        first(0, h, tn(decayed, v_v[:, cols(h)]))
    first_send(0)

    loads[3].wait()
    q_v[...] = q_v[...] * jnp.asarray(factor, BF16)
    for h in range(2):
        dq[:, cols(h)] = (q_v[:, cols(h)].astype(F32) * inc[h]).astype(BF16)
        cum_row, cum_col = cums[h]
        wt[h] = jnp.exp(jnp.where(same, cum_col - cum_row, -1e30))
        sm[h] = (nt(q_v[:, cols(h)], k_v[:, cols(h)]) * wt[h]).astype(BF16)
    loads[4].wait()
    acc[...] = nt(og_v[0], w_v[0])

    arrived(t_rec, members - 1, t_sem.at[1])
    second_send(0)

    for i in range(1, 4):
        loads[4 + i].wait()

    def add(slot, c):
        at = slice(c * chunk, (c + 1) * chunk)
        acc[at, :] += nt(og_v[slot, at], w_v[slot])

    half = CHUNKS // 2
    for c in range(half):
        to_right[c].wait_recv()
        onward[c].start()
        to_left[CHUNKS - 1 - c].wait_recv()
        onward[CHUNKS - 1 - c].start()
        add(1, c)
        add(2, CHUNKS - 1 - c)
        if c == 0:
            third_send(0)
    fourth_send(0)
    for c in range(half):
        to_right[half + c].wait_recv()
        add(1, half + c)
        to_left[half - 1 - c].wait_recv()
        add(2, half - 1 - c)

    adj = [jnp.zeros((size, size), F32), jnp.zeros((size, size), F32)]
    for c in range(half):
        for at in (c, CHUNKS - 1 - c):
            onward[at].wait_recv()
            span = slice(at * chunk, (at + 1) * chunk)
            here = (acc[span, :] + nt(og_v[3, span], w_v[3])).astype(BF16)
            g_v[span, :] = here
            for h in range(2):
                adj[h] = adj[h] + tn(dq[span, cols(h)], here[:, cols(h)])
    for h in range(2):
        first(1, h, adj[h])
    first_send(1)

    outs = []

    def put(src, dst, h, i):
        copy = pltpu.make_async_copy(src.at[:, cols(h)], dst.at[:, cols(h)], out_sem.at[i, h])
        copy.start()
        outs.append(copy)

    for h in range(2):
        fm[h] = (nt(g_v[:, cols(h)], v_v[:, cols(h)]) * wt[h]).astype(BF16)
    second_send(1)
    arrived(st_in.at[0], members - 1, c_rec.at[0, 3])
    for h in range(2):
        entering = nt(g_v[:, cols(h)], state(0, h))
        qg_v[:, cols(h)] = factor * (nn(fm[h], k_v[:, cols(h)]) + inc[h] * entering)
        put(qg_v, qg, h, 0)
    third_send(1)
    for h in range(2):
        kg_v[:, cols(h)] = tn(fm[h], q_v[:, cols(h)])
    fourth_send(1)
    for h in range(2):
        vg_v[:, cols(h)] = tn(sm[h], g_v[:, cols(h)])

    for copy in to_right + to_left + onward:
        copy.wait_send()
    arrived(t_rec, members - 1, t_sem.at[0])
    for direction in range(2):
        zs = za_send if direction else zf_send
        arrived(s_send.at[direction], members - 1, c_send.at[direction, 0])
        arrived(zs, planes - 1, c_send.at[direction, 1])
        arrived(zb_send.at[direction], planes - 1, c_send.at[direction, 2])
        arrived(o_send.at[direction], members - 1, c_send.at[direction, 3])

    arrived(st_in.at[1], members - 1, c_rec.at[1, 3])
    for h in range(2):
        kg_v[:, cols(h)] += outc[h] * nt(v_v[:, cols(h)], state(1, h))
        put(kg_v, kg, h, 1)
        vg_v[:, cols(h)] += outc[h] * nn(k_v[:, cols(h)], state(1, h))
        put(vg_v, vg, h, 2)
    for copy in outs:
        copy.wait()


def on_device(planes, members, out_grad, out_proj, query_rows, key_rows, value_rows, log_decay, doc_starts):
    tokens, width = query_rows.shape
    feats = out_grad.shape[1]
    size = width // 2
    rows = width // members
    sub = rows // planes
    any_space = pl.BlockSpec(memory_space=pl.ANY)
    result = jax.ShapeDtypeStruct((tokens, width), F32)
    lanes = 128
    scratch = [
        pltpu.VMEM((4, tokens, feats), BF16),
        pltpu.VMEM((4, width, feats), BF16),
        pltpu.VMEM((tokens, width), BF16),
        pltpu.VMEM((tokens, width), BF16),
        pltpu.VMEM((tokens, width), BF16),
        pltpu.VMEM((tokens, width), F32),
        pltpu.VMEM((tokens, width), BF16),
        pltpu.VMEM((2, tokens, tokens), F32),
        pltpu.VMEM((2, tokens, tokens), BF16),
        pltpu.VMEM((2, tokens, tokens), BF16),
        pltpu.VMEM((tokens, width), BF16),
        pltpu.VMEM((2, tokens, 1), F32),
        pltpu.VMEM((2, tokens, 1), F32),
        pltpu.VMEM((tokens, width), F32),
        pltpu.VMEM((tokens, width), F32),
        pltpu.VMEM((tokens, width), F32),
        pltpu.VMEM((2, 8, lanes), F32),
        pltpu.VMEM((members, 8, lanes), F32),
        pltpu.VMEM((2, members, rows, size), BF16),
        pltpu.VMEM((2, members, rows, size), BF16),
        pltpu.VMEM((2, members, rows, size), F32),
        pltpu.VMEM((planes, sub + 8, size), F32),
        pltpu.VMEM((planes, sub + 8, size), F32),
        pltpu.VMEM((planes, sub, size), F32),
        pltpu.VMEM((planes, sub, size), F32),
        pltpu.VMEM((2, planes, sub, size), F32),
        pltpu.VMEM((2, planes, sub, size), F32),
        pltpu.VMEM((2, members, rows, size), BF16),
        pltpu.VMEM((2, members, rows, size), BF16),
        pltpu.SemaphoreType.DMA((8,)),
        pltpu.SemaphoreType.DMA((3, 2)),
        pltpu.SemaphoreType.DMA((3, CHUNKS)),
        pltpu.SemaphoreType.DMA((3, CHUNKS)),
        pltpu.SemaphoreType.DMA((2,)),
        pltpu.SemaphoreType.DMA((2, 4)),
        pltpu.SemaphoreType.DMA((2, 4)),
    ]
    return pl.pallas_call(
        functools.partial(kernel, planes, members),
        out_shape=(result, result, result),
        in_specs=[
            pl.BlockSpec(memory_space=pltpu.SMEM),
            pl.BlockSpec(memory_space=pltpu.VMEM),
        ] + [any_space] * 5,
        out_specs=(any_space, any_space, any_space),
        scratch_shapes=scratch,
        compiler_params=pltpu.CompilerParams(
            collective_id=0, has_side_effects=True, vmem_limit_bytes=56 * 1024 * 1024
        ),
        name="retention_backward",
    )(doc_starts, log_decay, out_grad, out_proj, query_rows, key_rows, value_rows)


def solution(mesh):
    members = PLANE
    planes = mesh.shape["ctx"] // members
    return jax.shard_map(
        functools.partial(on_device, planes, members),
        mesh=mesh,
        in_specs=(
            P("ctx", "head"),
            P("head", None),
            P("ctx", "head"),
            P("ctx", "head"),
            P("ctx", "head"),
            P("head", "ctx"),
            P(),
        ),
        out_specs=(P("ctx", "head"), P("ctx", "head"), P("ctx", "head")),
        check_vma=False,
    )
```

```python
import functools

import jax
import jax.numpy as jnp
from jax import lax
from jax.experimental import pallas as pl
from jax.experimental.pallas import tpu as pltpu
from jax.sharding import PartitionSpec as P

PLANE = 4
CHUNKS = 4
MESH = pl.DeviceIdType.MESH
F32 = jnp.float32
BF16 = jnp.bfloat16


def nn(a, b):
    return lax.dot_general(a, b, (((1,), (0,)), ((), ())), preferred_element_type=F32)


def nt(a, b):
    return lax.dot_general(a, b, (((1,), (1,)), ((), ())), preferred_element_type=F32)


def tn(a, b):
    return lax.dot_general(a, b, (((0,), (0,)), ((), ())), preferred_element_type=F32)


def far_first(n, size):
    half = size // 2
    return half + lax.rem(n + 1, 2) * (n // 2) - lax.rem(n, 2) * ((n + 1) // 2)


def kernel(
    planes, lines,
    doc, ld, og, w, q, k, v,
    qg, kg, vg, adjoint, outflow,
    og_v, w_v, q_v, k_v, v_v, acc, g_v, wt, sm, fm, dq, inc, outc, qg_v, kg_v, vg_v, oc_v,
    t_send, t_other, tc_send, t_rec, own, core_send, core_rec, ch_send, ch_rec, en_send, en_rec,
    back_send, st_in,
    local_sem, out_sem, y_send, y_rec, t_sem, c_send, c_rec,
):
    tokens, width = q_v.shape
    feats = og_v.shape[2]
    size = width // 2
    chips, height, wide = ch_send.shape[1:]
    chunk = tokens // CHUNKS
    factor = size ** -0.5
    ctx, y = lax.axis_index("ctx"), lax.axis_index("head")
    chip, core = ctx // 2, ctx % 2
    z, x = chip // lines, chip % lines
    first_core = core == 0
    other = chip * 2 + 1 - core
    right, left = (y + 1) % 4, (y + 3) % 4
    owners = (y, left, right, (y + 2) % 4)

    loads = [pltpu.make_async_copy(og, og_v.at[0], local_sem.at[0])]
    for i, (src, dst) in enumerate(((k, k_v), (v, v_v), (q, q_v))):
        loads.append(pltpu.make_async_copy(src, dst, local_sem.at[1 + i]))
    for i in range(4):
        start = pl.multiple_of(owners[i] * feats, 128)
        loads.append(pltpu.make_async_copy(w.at[:, pl.ds(start, feats)], w_v.at[i], local_sem.at[4 + i]))
    for load in loads:
        load.start()

    def partner(n):
        there = (z + far_first(n // lines, planes)) % planes
        return there * lines + (x + far_first(n % lines, lines)) % lines

    barrier = pltpu.get_barrier_semaphore()

    def greet(n, c):
        pl.semaphore_signal(barrier, inc=1, device_id=(partner(n) * 2 + core, y), device_id_type=MESH)
        return c

    lax.fori_loop(0, chips - 1, greet, 0)
    for near in ((ctx, left), (ctx, right), (other, y)):
        pl.semaphore_signal(barrier, inc=1, device_id=near, device_id_type=MESH)
    pl.semaphore_wait(barrier, 3 + chips - 1)

    def hop(src_slot, dst_slot, c, to, lane):
        at = pl.ds(c * chunk, chunk)
        return pltpu.make_async_remote_copy(
            src_ref=og_v.at[src_slot, at], dst_ref=og_v.at[dst_slot, at],
            send_sem=y_send.at[lane, c], recv_sem=y_rec.at[dst_slot - 1, c],
            device_id=(ctx, to), device_id_type=MESH,
        )

    to_right = [hop(0, 1, c, right, 0) for c in range(CHUNKS)]
    to_left = [hop(0, 2, c, left, 1) for c in range(CHUNKS)]
    onward = [hop(1, 3, c, right, 2) if c < CHUNKS // 2 else hop(2, 3, c, left, 2) for c in range(CHUNKS)]
    loads[0].wait()
    for c in range(CHUNKS):
        to_right[c].start()
        to_left[CHUNKS - 1 - c].start()

    offset = ctx * tokens
    lane = lax.broadcasted_iota(jnp.int32, (8, tokens), 1)
    docs = [doc[i] for i in range(doc.shape[0])]

    def segment(places):
        total = jnp.zeros(places.shape, jnp.int32)
        for d in docs:
            total = total + (d <= places).astype(jnp.int32)
        return total

    def segment_at(place):
        total = jnp.int32(0)
        for d in docs:
            total = total + (d <= place).astype(jnp.int32)
        return total

    before, last = segment_at(offset - 1), segment_at(offset + tokens - 1)
    seg_row = segment(offset + lane)[0:1]
    row_at = lax.broadcasted_iota(jnp.int32, (tokens, tokens), 0)
    col_at = lax.broadcasted_iota(jnp.int32, (tokens, tokens), 1)
    seg_col = segment(offset + lax.broadcasted_iota(jnp.int32, (tokens, 1), 0))
    in_col = (seg_col == before).astype(F32)
    out_col = (seg_col == last).astype(F32)
    same = (seg_col == seg_row) & (col_at <= row_at)
    cums = []
    for h in range(2):
        cum = jnp.broadcast_to(ld[h : h + 1, :], (8, tokens))
        step = 1
        while step < tokens:
            cum = cum + jnp.where(lane >= step, pltpu.roll(cum, step, 1), 0.0)
            step *= 2
        whole = jnp.sum(jnp.where(lane == tokens - 1, cum, 0.0), axis=1, keepdims=True)
        through = jnp.exp(whole) * jnp.where(before == last, 1.0, 0.0)
        t_send[h] = jnp.broadcast_to(through, (8, t_send.shape[2]))
        cum_row = cum[0:1]
        cum_col = jnp.sum(jnp.where(row_at == col_at, cum_row, 0.0), axis=1, keepdims=True)
        inc[h] = jnp.exp(cum_col) * in_col
        outc[h] = jnp.exp(whole[0:1] - cum_col) * out_col
        cums.append((cum_row, cum_col))

    def to_core(src, dst, send, recv):
        return pltpu.make_async_remote_copy(
            src_ref=src, dst_ref=dst, send_sem=send, recv_sem=recv,
            device_id=(other, y), device_id_type=MESH,
        )

    def to_chips(src, dst, send, recv, index):
        def one(n, c):
            j = partner(n)
            pltpu.make_async_remote_copy(
                src_ref=src.at[index(j)], dst_ref=dst.at[chip], send_sem=send, recv_sem=recv,
                device_id=(j * 2 + core, y), device_id_type=MESH,
            ).start()
            return c

        lax.fori_loop(0, chips - 1, one, 0)

    def arrived(ref, count, sem):
        part = ref.at[pl.ds(0, count)]
        pltpu.make_async_copy(part, part, sem).wait()

    t_copy = to_core(t_send.at[1 - core], t_other, t_sem.at[0], t_sem.at[1])
    t_copy.start()

    def decay(ref):
        return ref[0:1, 0:1]

    def core_copy(direction):
        return to_core(
            core_send.at[direction], core_rec.at[direction], c_send.at[direction, 0], c_rec.at[direction, 0]
        )

    def back_copy(direction):
        return to_core(
            back_send.at[direction], st_in.at[direction, core], c_send.at[direction, 3], c_rec.at[direction, 3]
        )

    def first_send(direction):
        core_send[direction] = own[direction, 1 - core].astype(BF16)
        core_copy(direction).start()

    def pieces(ref, direction, whole):
        half = chips // 2 if chips > 1 else 1
        for i in range(2):
            part = whole[:, i * wide : (i + 1) * wide]
            ref[direction, i * half : (i + 1) * half] = part.reshape(half, height, wide)

    def second_send(direction):
        core_copy(direction).wait_recv()
        mine, theirs = own[direction, core], core_rec[direction].astype(F32)
        earlier = first_core if direction == 0 else jnp.logical_not(first_core)
        a = jnp.where(earlier, decay(t_other), 1.0)
        b = jnp.where(earlier, 1.0, decay(t_send.at[core]))
        pieces(ch_send, direction, (a * mine + b * theirs).astype(BF16))
        to_chips(
            ch_send.at[direction], ch_rec.at[direction], c_send.at[direction, 1], c_rec.at[direction, 1],
            lambda j: j,
        )
        ch_rec[direction, chip] = ch_send[direction, chip]

    def third_send(direction):
        arrived(ch_rec.at[direction], chips - 1, c_rec.at[direction, 1])
        run = jnp.zeros((height // 8, 8, wide), F32)
        for i in range(chips) if direction == 0 else reversed(range(chips)):
            en_send[direction, i] = run.reshape(height, wide).astype(BF16)
            here = ch_rec[direction, i].astype(F32).reshape(height // 8, 8, wide)
            run = t_rec[i, :, 0:wide] * run + here
        to_chips(
            en_send.at[direction], en_rec.at[direction], c_send.at[direction, 2], c_rec.at[direction, 2],
            lambda j: j,
        )
        en_rec[direction, chip] = en_send[direction, chip]

    def fourth_send(direction):
        arrived(en_rec.at[direction], chips - 1, c_rec.at[direction, 2])
        half = chips // 2
        parts = [en_rec[direction, i * half : (i + 1) * half].reshape(size, wide) for i in range(2)]
        entering = jnp.concatenate(parts, axis=1).astype(F32)
        earlier = first_core if direction == 0 else jnp.logical_not(first_core)
        a = jnp.where(earlier, decay(t_send.at[core]), 1.0)
        b = jnp.where(earlier, 1.0, 0.0)
        back_send[direction] = (a * entering + b * own[direction, core]).astype(BF16)
        back_copy(direction).start()
        a = jnp.where(earlier, 1.0, decay(t_other))
        st_in[direction, core] = (a * entering + (1.0 - b) * core_rec[direction].astype(F32)).astype(BF16)

    def cols(h):
        return slice(h * size, (h + 1) * size)

    loads[1].wait()
    loads[2].wait()
    for h in range(2):
        decayed = (k_v[:, cols(h)].astype(F32) * outc[h]).astype(BF16)
        own[0, h] = tn(decayed, v_v[:, cols(h)])
    first_send(0)
    t_copy.wait_recv()
    tc_send[...] = t_send[core] * t_other[...]
    to_chips(tc_send, t_rec, t_sem.at[2], t_sem.at[3], lambda j: slice(None))
    t_rec[chip] = tc_send[...]
    second_send(0)

    loads[3].wait()
    q_v[...] = q_v[...] * jnp.asarray(factor, BF16)
    at_lane = lax.broadcasted_iota(jnp.int32, oc_v.shape, 1)
    oc_v[...] = jnp.where(at_lane == 0, outc[0], outc[1])
    for h in range(2):
        dq[:, cols(h)] = (q_v[:, cols(h)].astype(F32) * inc[h]).astype(BF16)
        cum_row, cum_col = cums[h]
        wt[h] = jnp.exp(jnp.where(same, cum_col - cum_row, -1e30))
        sm[h] = (nt(q_v[:, cols(h)], k_v[:, cols(h)]) * wt[h]).astype(BF16)
    loads[4].wait()
    acc[...] = nt(og_v[0], w_v[0])
    for i in range(1, 4):
        loads[4 + i].wait()

    def add(slot, c):
        at = slice(c * chunk, (c + 1) * chunk)
        acc[at, :] += nt(og_v[slot, at], w_v[slot])

    half = CHUNKS // 2
    for c in range(half):
        to_right[c].wait_recv()
        onward[c].start()
        to_left[CHUNKS - 1 - c].wait_recv()
        onward[CHUNKS - 1 - c].start()
        add(1, c)
        add(2, CHUNKS - 1 - c)
        if c == 0:
            arrived(t_rec, chips - 1, t_sem.at[3])
            third_send(0)
    for c in range(half):
        to_right[half + c].wait_recv()
        add(1, half + c)
        to_left[half - 1 - c].wait_recv()
        add(2, half - 1 - c)
        if c == 0:
            fourth_send(0)

    adj = [jnp.zeros((size, size), F32), jnp.zeros((size, size), F32)]
    for c in range(half):
        for at in (c, CHUNKS - 1 - c):
            onward[at].wait_recv()
            span = slice(at * chunk, (at + 1) * chunk)
            here = (acc[span, :] + nt(og_v[3, span], w_v[3])).astype(BF16)
            g_v[span, :] = here
            for h in range(2):
                adj[h] = adj[h] + tn(dq[span, cols(h)], here[:, cols(h)])
    for h in range(2):
        own[1, h] = adj[h]
    first_send(1)

    outs = [pltpu.make_async_copy(oc_v, outflow, out_sem.at[3, 0])]
    outs[0].start()

    def put(src, dst, h, i):
        copy = pltpu.make_async_copy(src.at[:, cols(h)], dst.at[:, cols(h)], out_sem.at[i, h])
        copy.start()
        outs.append(copy)

    second_send(1)
    for h in range(2):
        fm[h] = (nt(g_v[:, cols(h)], v_v[:, cols(h)]) * wt[h]).astype(BF16)
    back_copy(0).wait_recv()
    for h in range(2):
        entering = nt(g_v[:, cols(h)], st_in[0, h])
        qg_v[:, cols(h)] = factor * (nn(fm[h], k_v[:, cols(h)]) + inc[h] * entering)
        put(qg_v, qg, h, 0)
    third_send(1)
    for h in range(2):
        kg_v[:, cols(h)] = tn(fm[h], q_v[:, cols(h)])
        put(kg_v, kg, h, 1)
        vg_v[:, cols(h)] = tn(sm[h], g_v[:, cols(h)])
        put(vg_v, vg, h, 2)

    for copy in to_right + to_left + onward + [t_copy]:
        copy.wait_send()
    arrived(t_rec, chips - 1, t_sem.at[2])
    for direction in range(2):
        core_copy(direction).wait_send()
        arrived(ch_send.at[direction], chips - 1, c_send.at[direction, 1])
    arrived(en_send.at[0], chips - 1, c_send.at[0, 2])
    back_copy(0).wait_send()

    fourth_send(1)
    arrived(en_send.at[1], chips - 1, c_send.at[1, 2])
    for copy in outs:
        copy.wait()
    back_copy(1).wait()
    last_copy = pltpu.make_async_copy(st_in.at[1], adjoint, out_sem.at[3, 1])
    last_copy.start()
    last_copy.wait()


def finish(adjoint, outflow, k, v, q_part, k_part, v_part, qg, kg, vg, a_v, o_v, k_v, v_v, kp, vp, sem, out_sem):
    tokens, width = k_v.shape
    size = width // 2
    half = tokens // 2
    through = pltpu.make_async_copy(q_part, qg, out_sem.at[2, 0])
    early = [
        pltpu.make_async_copy(src, dst, sem.at[0, i])
        for i, (src, dst) in enumerate(((adjoint, a_v), (outflow, o_v), (v, v_v), (k, k_v)))
    ]
    parts = []
    for c in range(2):
        at = pl.ds(c * half, half)
        for i, (src, dst) in enumerate(((k_part, kp), (v_part, vp))):
            parts.append(pltpu.make_async_copy(src.at[at], dst.at[at], sem.at[1 + i, c]))
    for copy in early + parts + [through]:
        copy.start()
    for copy in early:
        copy.wait()
    outs = []
    for c in range(2):
        at = slice(c * half, (c + 1) * half)
        rows = pl.ds(c * half, half)
        for i in range(2):
            parts[2 * c + i].wait()
            for h in range(2):
                cols = slice(h * size, (h + 1) * size)
                term = nn(k_v[at, cols], a_v[h]) if i else nt(v_v[at, cols], a_v[h])
                part = vp if i else kp
                part[at, cols] += o_v[at, h : h + 1] * term
            src, dst = (vp, vg) if i else (kp, kg)
            copy = pltpu.make_async_copy(src.at[rows], dst.at[rows], out_sem.at[i, c])
            copy.start()
            outs.append(copy)
    for copy in outs + [through]:
        copy.wait()


def on_device(planes, lines, out_grad, out_proj, query_rows, key_rows, value_rows, log_decay, doc_starts):
    tokens, width = query_rows.shape
    feats = out_grad.shape[1]
    size = width // 2
    chips = planes * lines
    height, wide = size * 2 // chips, size // 2
    any_space = pl.BlockSpec(memory_space=pl.ANY)
    result = jax.ShapeDtypeStruct((tokens, width), F32)
    adjoint = jax.ShapeDtypeStruct((2, size, size), BF16)
    outflow = jax.ShapeDtypeStruct((tokens, 128), F32)
    tile = (8, 128)
    scratch = [
        pltpu.VMEM((4, tokens, feats), BF16),
        pltpu.VMEM((4, width, feats), BF16),
        pltpu.VMEM((tokens, width), BF16),
        pltpu.VMEM((tokens, width), BF16),
        pltpu.VMEM((tokens, width), BF16),
        pltpu.VMEM((tokens, width), F32),
        pltpu.VMEM((tokens, width), BF16),
        pltpu.VMEM((2, tokens, tokens), F32),
        pltpu.VMEM((2, tokens, tokens), BF16),
        pltpu.VMEM((2, tokens, tokens), BF16),
        pltpu.VMEM((tokens, width), BF16),
        pltpu.VMEM((2, tokens, 1), F32),
        pltpu.VMEM((2, tokens, 1), F32),
        pltpu.VMEM((tokens, width), F32),
        pltpu.VMEM((tokens, width), F32),
        pltpu.VMEM((tokens, width), F32),
        pltpu.VMEM((tokens, 128), F32),
        pltpu.VMEM((2,) + tile, F32),
        pltpu.VMEM(tile, F32),
        pltpu.VMEM(tile, F32),
        pltpu.VMEM((chips,) + tile, F32),
        pltpu.VMEM((2, 2, size, size), F32),
        pltpu.VMEM((2, size, size), BF16),
        pltpu.VMEM((2, size, size), BF16),
        pltpu.VMEM((2, chips, height, wide), BF16),
        pltpu.VMEM((2, chips, height, wide), BF16),
        pltpu.VMEM((2, chips, height, wide), BF16),
        pltpu.VMEM((2, chips, height, wide), BF16),
        pltpu.VMEM((2, size, size), BF16),
        pltpu.VMEM((2, 2, size, size), BF16),
        pltpu.SemaphoreType.DMA((8,)),
        pltpu.SemaphoreType.DMA((4, 2)),
        pltpu.SemaphoreType.DMA((3, CHUNKS)),
        pltpu.SemaphoreType.DMA((3, CHUNKS)),
        pltpu.SemaphoreType.DMA((4,)),
        pltpu.SemaphoreType.DMA((2, 4)),
        pltpu.SemaphoreType.DMA((2, 4)),
    ]
    q_part, k_part, v_part, adjoint, outflow = pl.pallas_call(
        functools.partial(kernel, planes, lines),
        out_shape=(result, result, result, adjoint, outflow),
        in_specs=[
            pl.BlockSpec(memory_space=pltpu.SMEM),
            pl.BlockSpec(memory_space=pltpu.VMEM),
        ] + [pl.BlockSpec(memory_space=pltpu.HBM)] * 5,
        out_specs=(any_space,) * 5,
        scratch_shapes=scratch,
        compiler_params=pltpu.CompilerParams(
            collective_id=0, has_side_effects=True, vmem_limit_bytes=32 * 1024 * 1024
        ),
        name="retention_backward",
    )(doc_starts, log_decay, out_grad, out_proj, query_rows, key_rows, value_rows)
    return pl.pallas_call(
        finish,
        out_shape=(result, result, result),
        in_specs=[any_space] * 2 + [pl.BlockSpec(memory_space=pltpu.HBM)] * 2 + [any_space] * 3,
        out_specs=(any_space,) * 3,
        scratch_shapes=[
            pltpu.VMEM((2, size, size), BF16),
            pltpu.VMEM((tokens, 128), F32),
            pltpu.VMEM((tokens, width), BF16),
            pltpu.VMEM((tokens, width), BF16),
            pltpu.VMEM((tokens, width), F32),
            pltpu.VMEM((tokens, width), F32),
            pltpu.SemaphoreType.DMA((3, 4)),
            pltpu.SemaphoreType.DMA((3, 2)),
        ],
        compiler_params=pltpu.CompilerParams(vmem_limit_bytes=16 * 1024 * 1024),
        name="finish",
    )(adjoint, outflow, key_rows, value_rows, q_part, k_part, v_part)


def solution(mesh):
    lines = PLANE
    planes = mesh.shape["ctx"] // (2 * lines)
    return jax.shard_map(
        functools.partial(on_device, planes, lines),
        mesh=mesh,
        in_specs=(
            P("ctx", "head"),
            P("head", None),
            P("ctx", "head"),
            P("ctx", "head"),
            P("ctx", "head"),
            P("head", "ctx"),
            P(),
        ),
        out_specs=(P("ctx", "head"), P("ctx", "head"), P("ctx", "head")),
        check_vma=False,
    )
```

```python
import functools

import jax
import jax.numpy as jnp
from jax import lax
from jax.experimental import pallas as pl
from jax.experimental.pallas import tpu as pltpu
from jax.sharding import PartitionSpec as P

PLANE = 4
CHUNKS = 4
MESH = pl.DeviceIdType.MESH
F32 = jnp.float32
BF16 = jnp.bfloat16


def nn(a, b):
    return lax.dot_general(a, b, (((1,), (0,)), ((), ())), preferred_element_type=F32)


def nt(a, b):
    return lax.dot_general(a, b, (((1,), (1,)), ((), ())), preferred_element_type=F32)


def tn(a, b):
    return lax.dot_general(a, b, (((0,), (0,)), ((), ())), preferred_element_type=F32)


def far_first(n, size):
    half = size // 2
    return half + lax.rem(n + 1, 2) * (n // 2) - lax.rem(n, 2) * ((n + 1) // 2)


def kernel(
    planes, lines,
    doc, ld, og, w, q, k, v,
    qg, kg, vg, adjoint, outflow,
    og_v, w_v, q_v, k_v, v_v, acc, g_v, wt, sm, fm, dq, inc, outc, qg_v, kg_v, vg_v, oc_v,
    t_send, t_other, tc_send, t_rec, own, core_send, core_rec, ch_send, ch_rec, en_send, en_rec,
    back_send, st_in,
    local_sem, out_sem, y_send, y_rec, t_sem, c_send, c_rec,
):
    tokens, width = q_v.shape
    feats = og_v.shape[2]
    size = width // 2
    chips, height, wide = ch_send.shape[1:]
    chunk = tokens // CHUNKS
    factor = size ** -0.5
    ctx, y = lax.axis_index("ctx"), lax.axis_index("head")
    chip, core = ctx // 2, ctx % 2
    z, x = chip // lines, chip % lines
    first_core = core == 0
    other = chip * 2 + 1 - core
    right, left = (y + 1) % 4, (y + 3) % 4
    owners = (y, left, right, (y + 2) % 4)

    loads = [pltpu.make_async_copy(og, og_v.at[0], local_sem.at[0])]
    for i, (src, dst) in enumerate(((k, k_v), (v, v_v), (q, q_v))):
        loads.append(pltpu.make_async_copy(src, dst, local_sem.at[1 + i]))
    for i in range(4):
        start = pl.multiple_of(owners[i] * feats, 128)
        loads.append(pltpu.make_async_copy(w.at[:, pl.ds(start, feats)], w_v.at[i], local_sem.at[4 + i]))
    for load in loads:
        load.start()

    def partner(n):
        there = (z + far_first(n // lines, planes)) % planes
        return there * lines + (x + far_first(n % lines, lines)) % lines

    barrier = pltpu.get_barrier_semaphore()

    def greet(n, c):
        pl.semaphore_signal(barrier, inc=1, device_id=(partner(n) * 2 + core, y), device_id_type=MESH)
        return c

    lax.fori_loop(0, chips - 1, greet, 0)
    for near in ((ctx, left), (ctx, right), (other, y)):
        pl.semaphore_signal(barrier, inc=1, device_id=near, device_id_type=MESH)
    pl.semaphore_wait(barrier, 3 + chips - 1)

    def hop(src_slot, dst_slot, c, to, lane):
        at = pl.ds(c * chunk, chunk)
        return pltpu.make_async_remote_copy(
            src_ref=og_v.at[src_slot, at], dst_ref=og_v.at[dst_slot, at],
            send_sem=y_send.at[lane, c], recv_sem=y_rec.at[dst_slot - 1, c],
            device_id=(ctx, to), device_id_type=MESH,
        )

    to_right = [hop(0, 1, c, right, 0) for c in range(CHUNKS)]
    to_left = [hop(0, 2, c, left, 1) for c in range(CHUNKS)]
    onward = [hop(1, 3, c, right, 2) if c < CHUNKS // 2 else hop(2, 3, c, left, 2) for c in range(CHUNKS)]
    loads[0].wait()
    for c in range(CHUNKS):
        to_right[c].start()
        to_left[CHUNKS - 1 - c].start()

    offset = ctx * tokens
    lane = lax.broadcasted_iota(jnp.int32, (8, tokens), 1)
    docs = [doc[i] for i in range(doc.shape[0])]

    def segment(places):
        total = jnp.zeros(places.shape, jnp.int32)
        for d in docs:
            total = total + (d <= places).astype(jnp.int32)
        return total

    def segment_at(place):
        total = jnp.int32(0)
        for d in docs:
            total = total + (d <= place).astype(jnp.int32)
        return total

    before, last = segment_at(offset - 1), segment_at(offset + tokens - 1)
    seg_row = segment(offset + lane)[0:1]
    row_at = lax.broadcasted_iota(jnp.int32, (tokens, tokens), 0)
    col_at = lax.broadcasted_iota(jnp.int32, (tokens, tokens), 1)
    seg_col = segment(offset + lax.broadcasted_iota(jnp.int32, (tokens, 1), 0))
    in_col = (seg_col == before).astype(F32)
    out_col = (seg_col == last).astype(F32)
    same = (seg_col == seg_row) & (col_at <= row_at)
    cums = []
    for h in range(2):
        cum = jnp.broadcast_to(ld[h : h + 1, :], (8, tokens))
        step = 1
        while step < tokens:
            cum = cum + jnp.where(lane >= step, pltpu.roll(cum, step, 1), 0.0)
            step *= 2
        whole = jnp.sum(jnp.where(lane == tokens - 1, cum, 0.0), axis=1, keepdims=True)
        through = jnp.exp(whole) * jnp.where(before == last, 1.0, 0.0)
        t_send[h] = jnp.broadcast_to(through, (8, t_send.shape[2]))
        cum_row = cum[0:1]
        cum_col = jnp.sum(jnp.where(row_at == col_at, cum_row, 0.0), axis=1, keepdims=True)
        inc[h] = jnp.exp(cum_col) * in_col
        outc[h] = jnp.exp(whole[0:1] - cum_col) * out_col
        cums.append((cum_row, cum_col))

    def to_core(src, dst, send, recv):
        return pltpu.make_async_remote_copy(
            src_ref=src, dst_ref=dst, send_sem=send, recv_sem=recv,
            device_id=(other, y), device_id_type=MESH,
        )

    def to_chips(src, dst, send, recv, index):
        def one(n, c):
            j = partner(n)
            pltpu.make_async_remote_copy(
                src_ref=src.at[index(j)], dst_ref=dst.at[chip], send_sem=send, recv_sem=recv,
                device_id=(j * 2 + core, y), device_id_type=MESH,
            ).start()
            return c

        lax.fori_loop(0, chips - 1, one, 0)

    def arrived(ref, count, sem):
        part = ref.at[pl.ds(0, count)]
        pltpu.make_async_copy(part, part, sem).wait()

    t_copy = to_core(t_send.at[1 - core], t_other, t_sem.at[0], t_sem.at[1])
    t_copy.start()

    def decay(ref):
        return ref[0:1, 0:1]

    def core_copy(direction):
        return to_core(
            core_send.at[direction], core_rec.at[direction], c_send.at[direction, 0], c_rec.at[direction, 0]
        )

    def back_copy(direction):
        return to_core(
            back_send.at[direction], st_in.at[direction, core], c_send.at[direction, 3], c_rec.at[direction, 3]
        )

    def first_send(direction):
        core_send[direction] = own[direction, 1 - core].astype(BF16)
        core_copy(direction).start()

    def pieces(ref, direction, whole):
        half = chips // 2 if chips > 1 else 1
        for i in range(2):
            part = whole[:, i * wide : (i + 1) * wide]
            ref[direction, i * half : (i + 1) * half] = part.reshape(half, height, wide)

    def second_send(direction):
        core_copy(direction).wait_recv()
        mine, theirs = own[direction, core], core_rec[direction].astype(F32)
        earlier = first_core if direction == 0 else jnp.logical_not(first_core)
        a = jnp.where(earlier, decay(t_other), 1.0)
        b = jnp.where(earlier, 1.0, decay(t_send.at[core]))
        pieces(ch_send, direction, (a * mine + b * theirs).astype(BF16))
        to_chips(
            ch_send.at[direction], ch_rec.at[direction], c_send.at[direction, 1], c_rec.at[direction, 1],
            lambda j: j,
        )
        ch_rec[direction, chip] = ch_send[direction, chip]

    def third_send(direction):
        arrived(ch_rec.at[direction], chips - 1, c_rec.at[direction, 1])
        run = jnp.zeros((height // 8, 8, wide), F32)
        for i in range(chips) if direction == 0 else reversed(range(chips)):
            en_send[direction, i] = run.reshape(height, wide).astype(BF16)
            here = ch_rec[direction, i].astype(F32).reshape(height // 8, 8, wide)
            run = t_rec[i, :, 0:wide] * run + here
        to_chips(
            en_send.at[direction], en_rec.at[direction], c_send.at[direction, 2], c_rec.at[direction, 2],
            lambda j: j,
        )
        en_rec[direction, chip] = en_send[direction, chip]

    def fourth_send(direction):
        arrived(en_rec.at[direction], chips - 1, c_rec.at[direction, 2])
        half = chips // 2
        parts = [en_rec[direction, i * half : (i + 1) * half].reshape(size, wide) for i in range(2)]
        entering = jnp.concatenate(parts, axis=1).astype(F32)
        earlier = first_core if direction == 0 else jnp.logical_not(first_core)
        a = jnp.where(earlier, decay(t_send.at[core]), 1.0)
        b = jnp.where(earlier, 1.0, 0.0)
        back_send[direction] = (a * entering + b * own[direction, core]).astype(BF16)
        back_copy(direction).start()
        a = jnp.where(earlier, 1.0, decay(t_other))
        st_in[direction, core] = (a * entering + (1.0 - b) * core_rec[direction].astype(F32)).astype(BF16)

    def cols(h):
        return slice(h * size, (h + 1) * size)

    loads[1].wait()
    loads[2].wait()
    for h in range(2):
        decayed = (k_v[:, cols(h)].astype(F32) * outc[h]).astype(BF16)
        own[0, h] = tn(decayed, v_v[:, cols(h)])
    first_send(0)
    t_copy.wait_recv()
    tc_send[...] = t_send[core] * t_other[...]
    to_chips(tc_send, t_rec, t_sem.at[2], t_sem.at[3], lambda j: slice(None))
    t_rec[chip] = tc_send[...]
    second_send(0)

    loads[3].wait()
    q_v[...] = q_v[...] * jnp.asarray(factor, BF16)
    at_lane = lax.broadcasted_iota(jnp.int32, oc_v.shape, 1)
    oc_v[...] = jnp.where(at_lane == 0, outc[0], outc[1])
    for h in range(2):
        dq[:, cols(h)] = (q_v[:, cols(h)].astype(F32) * inc[h]).astype(BF16)
        cum_row, cum_col = cums[h]
        wt[h] = jnp.exp(jnp.where(same, cum_col - cum_row, -1e30))
        sm[h] = (nt(q_v[:, cols(h)], k_v[:, cols(h)]) * wt[h]).astype(BF16)
    loads[4].wait()
    acc[...] = nt(og_v[0], w_v[0])
    for i in range(1, 4):
        loads[4 + i].wait()

    def add(slot, c):
        at = slice(c * chunk, (c + 1) * chunk)
        acc[at, :] += nt(og_v[slot, at], w_v[slot])

    half = CHUNKS // 2
    for c in range(half):
        to_right[c].wait_recv()
        onward[c].start()
        to_left[CHUNKS - 1 - c].wait_recv()
        onward[CHUNKS - 1 - c].start()
        add(1, c)
        add(2, CHUNKS - 1 - c)
        if c == 0:
            arrived(t_rec, chips - 1, t_sem.at[3])
            third_send(0)
    for c in range(half):
        to_right[half + c].wait_recv()
        add(1, half + c)
        to_left[half - 1 - c].wait_recv()
        add(2, half - 1 - c)
        if c == 0:
            fourth_send(0)

    adj = [jnp.zeros((size, size), F32), jnp.zeros((size, size), F32)]
    for c in range(half):
        for at in (c, CHUNKS - 1 - c):
            onward[at].wait_recv()
            span = slice(at * chunk, (at + 1) * chunk)
            here = (acc[span, :] + nt(og_v[3, span], w_v[3])).astype(BF16)
            g_v[span, :] = here
            for h in range(2):
                adj[h] = adj[h] + tn(dq[span, cols(h)], here[:, cols(h)])
    for h in range(2):
        own[1, h] = adj[h]
    first_send(1)

    outs = [pltpu.make_async_copy(oc_v, outflow, out_sem.at[3, 0])]
    outs[0].start()

    def put(src, dst, h, i):
        copy = pltpu.make_async_copy(src.at[:, cols(h)], dst.at[:, cols(h)], out_sem.at[i, h])
        copy.start()
        outs.append(copy)

    second_send(1)
    for h in range(2):
        fm[h] = (nt(g_v[:, cols(h)], v_v[:, cols(h)]) * wt[h]).astype(BF16)
    back_copy(0).wait_recv()
    for h in range(2):
        entering = nt(g_v[:, cols(h)], st_in[0, h])
        qg_v[:, cols(h)] = factor * (nn(fm[h], k_v[:, cols(h)]) + inc[h] * entering)
        put(qg_v, qg, h, 0)
    third_send(1)
    for h in range(2):
        kg_v[:, cols(h)] = tn(fm[h], q_v[:, cols(h)])
        put(kg_v, kg, h, 1)
        vg_v[:, cols(h)] = tn(sm[h], g_v[:, cols(h)])
        put(vg_v, vg, h, 2)

    for copy in to_right + to_left + onward + [t_copy]:
        copy.wait_send()
    arrived(t_rec, chips - 1, t_sem.at[2])
    for direction in range(2):
        core_copy(direction).wait_send()
        arrived(ch_send.at[direction], chips - 1, c_send.at[direction, 1])
    arrived(en_send.at[0], chips - 1, c_send.at[0, 2])
    back_copy(0).wait_send()

    fourth_send(1)
    arrived(en_send.at[1], chips - 1, c_send.at[1, 2])
    for copy in outs:
        copy.wait()
    back_copy(1).wait()
    last_copy = pltpu.make_async_copy(st_in.at[1], adjoint, out_sem.at[3, 1])
    last_copy.start()
    last_copy.wait()


def finish(adjoint, outflow, k, v, q_part, k_part, v_part, qg, kg, vg, a_v, o_v, k_v, v_v, kp, vp, sem, out_sem):
    tokens, width = k_v.shape
    size = width // 2
    half = tokens // 2
    through = pltpu.make_async_copy(q_part, qg, out_sem.at[2, 0])
    early = [
        pltpu.make_async_copy(src, dst, sem.at[0, i])
        for i, (src, dst) in enumerate(((adjoint, a_v), (outflow, o_v), (v, v_v), (k, k_v)))
    ]
    parts = []
    for c in range(2):
        at = pl.ds(c * half, half)
        for i, (src, dst) in enumerate(((k_part, kp), (v_part, vp))):
            parts.append(pltpu.make_async_copy(src.at[at], dst.at[at], sem.at[1 + i, c]))
    for copy in early + parts + [through]:
        copy.start()
    for copy in early:
        copy.wait()
    outs = []
    for c in range(2):
        at = slice(c * half, (c + 1) * half)
        rows = pl.ds(c * half, half)
        for i in range(2):
            parts[2 * c + i].wait()
            for h in range(2):
                cols = slice(h * size, (h + 1) * size)
                term = nn(k_v[at, cols], a_v[h]) if i else nt(v_v[at, cols], a_v[h])
                part = vp if i else kp
                part[at, cols] += o_v[at, h : h + 1] * term
            src, dst = (vp, vg) if i else (kp, kg)
            copy = pltpu.make_async_copy(src.at[rows], dst.at[rows], out_sem.at[i, c])
            copy.start()
            outs.append(copy)
    for copy in outs + [through]:
        copy.wait()


def on_device(planes, lines, out_grad, out_proj, query_rows, key_rows, value_rows, log_decay, doc_starts):
    tokens, width = query_rows.shape
    feats = out_grad.shape[1]
    size = width // 2
    chips = planes * lines
    height, wide = size * 2 // chips, size // 2
    any_space = pl.BlockSpec(memory_space=pl.ANY)
    result = jax.ShapeDtypeStruct((tokens, width), F32)
    adjoint = jax.ShapeDtypeStruct((2, size, size), BF16)
    outflow = jax.ShapeDtypeStruct((tokens, 128), F32)
    tile = (8, 128)
    scratch = [
        pltpu.VMEM((4, tokens, feats), BF16),
        pltpu.VMEM((4, width, feats), BF16),
        pltpu.VMEM((tokens, width), BF16),
        pltpu.VMEM((tokens, width), BF16),
        pltpu.VMEM((tokens, width), BF16),
        pltpu.VMEM((tokens, width), F32),
        pltpu.VMEM((tokens, width), BF16),
        pltpu.VMEM((2, tokens, tokens), F32),
        pltpu.VMEM((2, tokens, tokens), BF16),
        pltpu.VMEM((2, tokens, tokens), BF16),
        pltpu.VMEM((tokens, width), BF16),
        pltpu.VMEM((2, tokens, 1), F32),
        pltpu.VMEM((2, tokens, 1), F32),
        pltpu.VMEM((tokens, width), F32),
        pltpu.VMEM((tokens, width), F32),
        pltpu.VMEM((tokens, width), F32),
        pltpu.VMEM((tokens, 128), F32),
        pltpu.VMEM((2,) + tile, F32),
        pltpu.VMEM(tile, F32),
        pltpu.VMEM(tile, F32),
        pltpu.VMEM((chips,) + tile, F32),
        pltpu.VMEM((2, 2, size, size), F32),
        pltpu.VMEM((2, size, size), BF16),
        pltpu.VMEM((2, size, size), BF16),
        pltpu.VMEM((2, chips, height, wide), BF16),
        pltpu.VMEM((2, chips, height, wide), BF16),
        pltpu.VMEM((2, chips, height, wide), BF16),
        pltpu.VMEM((2, chips, height, wide), BF16),
        pltpu.VMEM((2, size, size), BF16),
        pltpu.VMEM((2, 2, size, size), BF16),
        pltpu.SemaphoreType.DMA((8,)),
        pltpu.SemaphoreType.DMA((4, 2)),
        pltpu.SemaphoreType.DMA((3, CHUNKS)),
        pltpu.SemaphoreType.DMA((3, CHUNKS)),
        pltpu.SemaphoreType.DMA((4,)),
        pltpu.SemaphoreType.DMA((2, 4)),
        pltpu.SemaphoreType.DMA((2, 4)),
    ]
    q_part, k_part, v_part, adjoint, outflow = pl.pallas_call(
        functools.partial(kernel, planes, lines),
        out_shape=tuple(pltpu.VMEM(a.shape, a.dtype) for a in (result, result, result, adjoint, outflow)),
        in_specs=[
            pl.BlockSpec(memory_space=pltpu.SMEM),
            pl.BlockSpec(memory_space=pltpu.VMEM),
        ] + [any_space] * 5,
        out_specs=(any_space,) * 5,
        scratch_shapes=scratch,
        compiler_params=pltpu.CompilerParams(
            collective_id=0, has_side_effects=True, vmem_limit_bytes=32 * 1024 * 1024
        ),
        name="retention_backward",
    )(*(
        pltpu.with_memory_space_constraint(a, pltpu.HBM)
        for a in (doc_starts, log_decay, out_grad, out_proj, query_rows, key_rows, value_rows)
    ))
    key_rows, value_rows = (pltpu.with_memory_space_constraint(a, pltpu.HBM) for a in (key_rows, value_rows))
    return pl.pallas_call(
        finish,
        out_shape=(result, result, result),
        in_specs=[any_space] * 7,
        out_specs=(any_space,) * 3,
        scratch_shapes=[
            pltpu.VMEM((2, size, size), BF16),
            pltpu.VMEM((tokens, 128), F32),
            pltpu.VMEM((tokens, width), BF16),
            pltpu.VMEM((tokens, width), BF16),
            pltpu.VMEM((tokens, width), F32),
            pltpu.VMEM((tokens, width), F32),
            pltpu.SemaphoreType.DMA((3, 4)),
            pltpu.SemaphoreType.DMA((3, 2)),
        ],
        compiler_params=pltpu.CompilerParams(vmem_limit_bytes=16 * 1024 * 1024),
        name="finish",
    )(adjoint, outflow, key_rows, value_rows, q_part, k_part, v_part)


def solution(mesh):
    lines = PLANE
    planes = mesh.shape["ctx"] // (2 * lines)
    return jax.shard_map(
        functools.partial(on_device, planes, lines),
        mesh=mesh,
        in_specs=(
            P("ctx", "head"),
            P("head", None),
            P("ctx", "head"),
            P("ctx", "head"),
            P("ctx", "head"),
            P("head", "ctx"),
            P(),
        ),
        out_specs=(P("ctx", "head"), P("ctx", "head"), P("ctx", "head")),
        check_vma=False,
    )
```

```python
import functools

import jax
import jax.numpy as jnp
from jax import lax
from jax.experimental import pallas as pl
from jax.experimental.pallas import tpu as pltpu
from jax.sharding import PartitionSpec as P

PLANE = 4
CHUNKS = 4
MESH = pl.DeviceIdType.MESH
F32 = jnp.float32
BF16 = jnp.bfloat16


def nn(a, b):
    return lax.dot_general(a, b, (((1,), (0,)), ((), ())), preferred_element_type=F32)


def nt(a, b):
    return lax.dot_general(a, b, (((1,), (1,)), ((), ())), preferred_element_type=F32)


def tn(a, b):
    return lax.dot_general(a, b, (((0,), (0,)), ((), ())), preferred_element_type=F32)


def far_first(n, size):
    half = size // 2
    return half + lax.rem(n + 1, 2) * (n // 2) - lax.rem(n, 2) * ((n + 1) // 2)


def ring_offsets(distance, size):
    return sorted({distance % size, -distance % size} - {0})


def kernel(
    planes, lines,
    doc, ld, og, w, q, k, v,
    qg, kg, vg, adjoint, outflow, k_out, v_out,
    og_v, w_v, q_v, k_v, v_v, acc, g_v, wt, sm, fm, dq, inc, outc, qg_v, kg_v, vg_v, oc_v,
    t_send, t_other, tc_send, t_rec, own, core_send, core_rec, ch_send, ch_rec, en_send, en_rec,
    back_send, st_in,
    local_sem, out_sem, y_send, y_rec, t_sem, c_send, c_rec, greet_sem,
):
    tokens, width = q_v.shape
    feats = og_v.shape[2]
    size = width // 2
    chips, height, wide = ch_send.shape[1:]
    chunk = tokens // CHUNKS
    factor = size ** -0.5
    ctx, y = lax.axis_index("ctx"), lax.axis_index("head")
    chip, core = ctx // 2, ctx % 2
    z, x = chip // lines, chip % lines
    first_core = core == 0
    other = chip * 2 + 1 - core
    right, left = (y + 1) % 4, (y + 3) % 4
    owners = (y, left, right, (y + 2) % 4)

    loads = [pltpu.make_async_copy(og, og_v.at[0], local_sem.at[0])]
    for i, (src, dst) in enumerate(((k, k_v), (v, v_v), (q, q_v))):
        loads.append(pltpu.make_async_copy(src, dst, local_sem.at[1 + i]))
    for i in range(4):
        start = pl.multiple_of(owners[i] * feats, 128)
        loads.append(pltpu.make_async_copy(w.at[:, pl.ds(start, feats)], w_v.at[i], local_sem.at[4 + i]))
    for load in loads:
        load.start()

    def partner(n):
        there = (z + far_first(n // lines, planes)) % planes
        return there * lines + (x + far_first(n % lines, lines)) % lines

    def at_chip(dz, dx):
        return (((z + dz) % planes * lines + (x + dx) % lines) * 2 + core, y)

    near_z, far_z = ring_offsets(1, planes), ring_offsets(2, planes)
    near_x = [at_chip(0, d) for d in ring_offsets(1, lines)]
    near_z, far_z = [at_chip(d, 0) for d in near_z], [at_chip(d, 0) for d in far_z]
    rounds = [near_z + near_x, near_z + far_z, far_z]
    barrier = pltpu.get_barrier_semaphore()
    entry = [(ctx, left), (ctx, right), (other, y)] + near_z + near_x
    for near in entry:
        pl.semaphore_signal(barrier, inc=1, device_id=near, device_id_type=MESH)
    pl.semaphore_wait(barrier, len(entry))

    def tell(i):
        for to in rounds[i]:
            pl.semaphore_signal(greet_sem.at[i], inc=1, device_id=to, device_id_type=MESH)

    def hear(i):
        if rounds[i]:
            pl.semaphore_wait(greet_sem.at[i], len(rounds[i]))

    def hop(src_slot, dst_slot, c, to, lane):
        at = pl.ds(c * chunk, chunk)
        return pltpu.make_async_remote_copy(
            src_ref=og_v.at[src_slot, at], dst_ref=og_v.at[dst_slot, at],
            send_sem=y_send.at[lane, c], recv_sem=y_rec.at[dst_slot - 1, c],
            device_id=(ctx, to), device_id_type=MESH,
        )

    to_right = [hop(0, 1, c, right, 0) for c in range(CHUNKS)]
    to_left = [hop(0, 2, c, left, 1) for c in range(CHUNKS)]
    onward = [hop(1, 3, c, right, 2) if c < CHUNKS // 2 else hop(2, 3, c, left, 2) for c in range(CHUNKS)]
    loads[0].wait()
    for c in range(CHUNKS):
        to_right[c].start()
        to_left[CHUNKS - 1 - c].start()
    tell(0)

    offset = ctx * tokens
    lane = lax.broadcasted_iota(jnp.int32, (8, tokens), 1)
    docs = [doc[i] for i in range(doc.shape[0])]

    def segment(places):
        total = jnp.zeros(places.shape, jnp.int32)
        for d in docs:
            total = total + (d <= places).astype(jnp.int32)
        return total

    def segment_at(place):
        total = jnp.int32(0)
        for d in docs:
            total = total + (d <= place).astype(jnp.int32)
        return total

    before, last = segment_at(offset - 1), segment_at(offset + tokens - 1)
    seg_row = segment(offset + lane)[0:1]
    row_at = lax.broadcasted_iota(jnp.int32, (tokens, tokens), 0)
    col_at = lax.broadcasted_iota(jnp.int32, (tokens, tokens), 1)
    seg_col = segment(offset + lax.broadcasted_iota(jnp.int32, (tokens, 1), 0))
    in_col = (seg_col == before).astype(F32)
    out_col = (seg_col == last).astype(F32)
    same = (seg_col == seg_row) & (col_at <= row_at)
    cums = []
    for h in range(2):
        cum = jnp.broadcast_to(ld[h : h + 1, :], (8, tokens))
        step = 1
        while step < tokens:
            cum = cum + jnp.where(lane >= step, pltpu.roll(cum, step, 1), 0.0)
            step *= 2
        whole = jnp.sum(jnp.where(lane == tokens - 1, cum, 0.0), axis=1, keepdims=True)
        through = jnp.exp(whole) * jnp.where(before == last, 1.0, 0.0)
        t_send[h] = jnp.broadcast_to(through, (8, t_send.shape[2]))
        cum_row = cum[0:1]
        cum_col = jnp.sum(jnp.where(row_at == col_at, cum_row, 0.0), axis=1, keepdims=True)
        inc[h] = jnp.exp(cum_col) * in_col
        outc[h] = jnp.exp(whole[0:1] - cum_col) * out_col
        cums.append((cum_row, cum_col))

    def to_core(src, dst, send, recv):
        return pltpu.make_async_remote_copy(
            src_ref=src, dst_ref=dst, send_sem=send, recv_sem=recv,
            device_id=(other, y), device_id_type=MESH,
        )

    def to_chips(src, dst, send, recv, index):
        def one(n, c):
            j = partner(n)
            pltpu.make_async_remote_copy(
                src_ref=src.at[index(j)], dst_ref=dst.at[chip], send_sem=send, recv_sem=recv,
                device_id=(j * 2 + core, y), device_id_type=MESH,
            ).start()
            return c

        lax.fori_loop(0, chips - 1, one, 0)

    def arrived(ref, count, sem):
        part = ref.at[pl.ds(0, count)]
        pltpu.make_async_copy(part, part, sem).wait()

    t_copy = to_core(t_send.at[1 - core], t_other, t_sem.at[0], t_sem.at[1])
    t_copy.start()

    def decay(ref):
        return ref[0:1, 0:1]

    def core_copy(direction):
        return to_core(
            core_send.at[direction], core_rec.at[direction], c_send.at[direction, 0], c_rec.at[direction, 0]
        )

    def back_copy(direction):
        return to_core(
            back_send.at[direction], st_in.at[direction, core], c_send.at[direction, 3], c_rec.at[direction, 3]
        )

    def first_send(direction):
        core_send[direction] = own[direction, 1 - core].astype(BF16)
        core_copy(direction).start()

    def pieces(ref, direction, whole):
        half = chips // 2 if chips > 1 else 1
        for i in range(2):
            part = whole[:, i * wide : (i + 1) * wide]
            ref[direction, i * half : (i + 1) * half] = part.reshape(half, height, wide)

    def second_send(direction):
        core_copy(direction).wait_recv()
        mine, theirs = own[direction, core], core_rec[direction].astype(F32)
        earlier = first_core if direction == 0 else jnp.logical_not(first_core)
        a = jnp.where(earlier, decay(t_other), 1.0)
        b = jnp.where(earlier, 1.0, decay(t_send.at[core]))
        pieces(ch_send, direction, (a * mine + b * theirs).astype(BF16))
        to_chips(
            ch_send.at[direction], ch_rec.at[direction], c_send.at[direction, 1], c_rec.at[direction, 1],
            lambda j: j,
        )
        ch_rec[direction, chip] = ch_send[direction, chip]

    def third_send(direction):
        arrived(ch_rec.at[direction], chips - 1, c_rec.at[direction, 1])
        run = jnp.zeros((height // 8, 8, wide), F32)
        for i in range(chips) if direction == 0 else reversed(range(chips)):
            en_send[direction, i] = run.reshape(height, wide).astype(BF16)
            here = ch_rec[direction, i].astype(F32).reshape(height // 8, 8, wide)
            run = t_rec[i, :, 0:wide] * run + here
        to_chips(
            en_send.at[direction], en_rec.at[direction], c_send.at[direction, 2], c_rec.at[direction, 2],
            lambda j: j,
        )
        en_rec[direction, chip] = en_send[direction, chip]

    def fourth_send(direction):
        arrived(en_rec.at[direction], chips - 1, c_rec.at[direction, 2])
        half = chips // 2
        parts = [en_rec[direction, i * half : (i + 1) * half].reshape(size, wide) for i in range(2)]
        entering = jnp.concatenate(parts, axis=1).astype(F32)
        earlier = first_core if direction == 0 else jnp.logical_not(first_core)
        a = jnp.where(earlier, decay(t_send.at[core]), 1.0)
        b = jnp.where(earlier, 1.0, 0.0)
        back_send[direction] = (a * entering + b * own[direction, core]).astype(BF16)
        back_copy(direction).start()
        a = jnp.where(earlier, 1.0, decay(t_other))
        st_in[direction, core] = (a * entering + (1.0 - b) * core_rec[direction].astype(F32)).astype(BF16)

    def cols(h):
        return slice(h * size, (h + 1) * size)

    loads[1].wait()
    loads[2].wait()
    for h in range(2):
        decayed = (k_v[:, cols(h)].astype(F32) * outc[h]).astype(BF16)
        own[0, h] = tn(decayed, v_v[:, cols(h)])
    first_send(0)
    hear(0)
    tell(1)

    loads[3].wait()
    q_v[...] = q_v[...] * jnp.asarray(factor, BF16)
    at_lane = lax.broadcasted_iota(jnp.int32, oc_v.shape, 1)
    oc_v[...] = jnp.where(at_lane == 0, outc[0], outc[1])
    for h in range(2):
        dq[:, cols(h)] = (q_v[:, cols(h)].astype(F32) * inc[h]).astype(BF16)
        cum_row, cum_col = cums[h]
        wt[h] = jnp.exp(jnp.where(same, cum_col - cum_row, -1e30))
        sm[h] = (nt(q_v[:, cols(h)], k_v[:, cols(h)]) * wt[h]).astype(BF16)
    hear(1)
    tell(2)
    loads[4].wait()
    acc[...] = nt(og_v[0], w_v[0])
    for i in range(1, 4):
        loads[4 + i].wait()
    hear(2)
    t_copy.wait_recv()
    tc_send[...] = t_send[core] * t_other[...]
    to_chips(tc_send, t_rec, t_sem.at[2], t_sem.at[3], lambda j: slice(None))
    t_rec[chip] = tc_send[...]
    second_send(0)

    def add(slot, c):
        at = slice(c * chunk, (c + 1) * chunk)
        acc[at, :] += nt(og_v[slot, at], w_v[slot])

    half = CHUNKS // 2
    for c in range(half):
        to_right[c].wait_recv()
        onward[c].start()
        to_left[CHUNKS - 1 - c].wait_recv()
        onward[CHUNKS - 1 - c].start()
        add(1, c)
        add(2, CHUNKS - 1 - c)
    for c in range(half):
        to_right[half + c].wait_recv()
        add(1, half + c)
        to_left[half - 1 - c].wait_recv()
        add(2, half - 1 - c)
    arrived(t_rec, chips - 1, t_sem.at[3])
    third_send(0)

    adj = [jnp.zeros((size, size), F32), jnp.zeros((size, size), F32)]
    for c in range(half):
        for at in (c, CHUNKS - 1 - c):
            onward[at].wait_recv()
            span = slice(at * chunk, (at + 1) * chunk)
            here = (acc[span, :] + nt(og_v[3, span], w_v[3])).astype(BF16)
            g_v[span, :] = here
            for h in range(2):
                adj[h] = adj[h] + tn(dq[span, cols(h)], here[:, cols(h)])
    for h in range(2):
        own[1, h] = adj[h]
    first_send(1)
    fourth_send(0)

    outs = [pltpu.make_async_copy(oc_v, outflow, out_sem.at[3, 0])]
    for i, (src, dst) in enumerate(((k_v, k_out), (v_v, v_out))):
        outs.append(pltpu.make_async_copy(src, dst, out_sem.at[4, i]))
    for copy in outs:
        copy.start()

    def put(src, dst, h, i):
        copy = pltpu.make_async_copy(src.at[:, cols(h)], dst.at[:, cols(h)], out_sem.at[i, h])
        copy.start()
        outs.append(copy)

    second_send(1)
    for h in range(2):
        fm[h] = (nt(g_v[:, cols(h)], v_v[:, cols(h)]) * wt[h]).astype(BF16)
    back_copy(0).wait_recv()
    for h in range(2):
        entering = nt(g_v[:, cols(h)], st_in[0, h])
        qg_v[:, cols(h)] = factor * (nn(fm[h], k_v[:, cols(h)]) + inc[h] * entering)
        put(qg_v, qg, h, 0)
    third_send(1)
    for h in range(2):
        kg_v[:, cols(h)] = tn(fm[h], q_v[:, cols(h)])
        put(kg_v, kg, h, 1)
        vg_v[:, cols(h)] = tn(sm[h], g_v[:, cols(h)])
        put(vg_v, vg, h, 2)

    for copy in to_right + to_left + onward + [t_copy]:
        copy.wait_send()
    arrived(t_rec, chips - 1, t_sem.at[2])
    for direction in range(2):
        core_copy(direction).wait_send()
        arrived(ch_send.at[direction], chips - 1, c_send.at[direction, 1])
    arrived(en_send.at[0], chips - 1, c_send.at[0, 2])
    back_copy(0).wait_send()

    fourth_send(1)
    arrived(en_send.at[1], chips - 1, c_send.at[1, 2])
    for copy in outs:
        copy.wait()
    back_copy(1).wait()
    last_copy = pltpu.make_async_copy(st_in.at[1], adjoint, out_sem.at[3, 1])
    last_copy.start()
    last_copy.wait()


def finish(adjoint, outflow, k, v, k_part, v_part, q_part, qg, kg, vg, k_all, v_all, sem):
    tokens, width = k.shape
    size = width // 2
    step = tokens // 4
    outs = [pltpu.make_async_copy(q_part, qg, sem.at[2, 0])]
    outs[0].start()
    for c in range(4):
        at = slice(c * step, (c + 1) * step)
        rows = pl.ds(c * step, step)
        for i, (part, whole, out) in enumerate(((k_part, k_all, kg), (v_part, v_all, vg))):
            for h in range(2):
                cols = slice(h * size, (h + 1) * size)
                term = nn(k[at, cols], adjoint[h]) if i else nt(v[at, cols], adjoint[h])
                whole[at, cols] = part[at, cols] + outflow[at, h : h + 1] * term
            copy = pltpu.make_async_copy(whole.at[rows], out.at[rows], sem.at[i, c])
            copy.start()
            outs.append(copy)
    for copy in outs:
        copy.wait()


def on_device(planes, lines, out_grad, out_proj, query_rows, key_rows, value_rows, log_decay, doc_starts):
    tokens, width = query_rows.shape
    feats = out_grad.shape[1]
    size = width // 2
    chips = planes * lines
    height, wide = size * 2 // chips, size // 2
    any_space = pl.BlockSpec(memory_space=pl.ANY)
    result = jax.ShapeDtypeStruct((tokens, width), F32)
    adjoint = jax.ShapeDtypeStruct((2, size, size), BF16)
    outflow = jax.ShapeDtypeStruct((tokens, 128), F32)
    tile = (8, 128)
    scratch = [
        pltpu.VMEM((4, tokens, feats), BF16),
        pltpu.VMEM((4, width, feats), BF16),
        pltpu.VMEM((tokens, width), BF16),
        pltpu.VMEM((tokens, width), BF16),
        pltpu.VMEM((tokens, width), BF16),
        pltpu.VMEM((tokens, width), F32),
        pltpu.VMEM((tokens, width), BF16),
        pltpu.VMEM((2, tokens, tokens), F32),
        pltpu.VMEM((2, tokens, tokens), BF16),
        pltpu.VMEM((2, tokens, tokens), BF16),
        pltpu.VMEM((tokens, width), BF16),
        pltpu.VMEM((2, tokens, 1), F32),
        pltpu.VMEM((2, tokens, 1), F32),
        pltpu.VMEM((tokens, width), F32),
        pltpu.VMEM((tokens, width), F32),
        pltpu.VMEM((tokens, width), F32),
        pltpu.VMEM((tokens, 128), F32),
        pltpu.VMEM((2,) + tile, F32),
        pltpu.VMEM(tile, F32),
        pltpu.VMEM(tile, F32),
        pltpu.VMEM((chips,) + tile, F32),
        pltpu.VMEM((2, 2, size, size), F32),
        pltpu.VMEM((2, size, size), BF16),
        pltpu.VMEM((2, size, size), BF16),
        pltpu.VMEM((2, chips, height, wide), BF16),
        pltpu.VMEM((2, chips, height, wide), BF16),
        pltpu.VMEM((2, chips, height, wide), BF16),
        pltpu.VMEM((2, chips, height, wide), BF16),
        pltpu.VMEM((2, size, size), BF16),
        pltpu.VMEM((2, 2, size, size), BF16),
        pltpu.SemaphoreType.DMA((8,)),
        pltpu.SemaphoreType.DMA((5, 2)),
        pltpu.SemaphoreType.DMA((3, CHUNKS)),
        pltpu.SemaphoreType.DMA((3, CHUNKS)),
        pltpu.SemaphoreType.DMA((4,)),
        pltpu.SemaphoreType.DMA((2, 4)),
        pltpu.SemaphoreType.DMA((2, 4)),
        pltpu.SemaphoreType.REGULAR((3,)),
    ]
    q_part, k_part, v_part, adjoint, outflow, key_rows, value_rows = pl.pallas_call(
        functools.partial(kernel, planes, lines),
        out_shape=tuple(pltpu.VMEM(a.shape, a.dtype) for a in (result, result, result, adjoint, outflow, key_rows, value_rows)),
        in_specs=[
            pl.BlockSpec(memory_space=pltpu.SMEM),
            pl.BlockSpec(memory_space=pltpu.VMEM),
        ] + [any_space] * 5,
        out_specs=(any_space,) * 7,
        scratch_shapes=scratch,
        compiler_params=pltpu.CompilerParams(
            collective_id=0, has_side_effects=True, vmem_limit_bytes=32 * 1024 * 1024
        ),
        name="retention_backward",
    )(*(
        pltpu.with_memory_space_constraint(a, pltpu.HBM)
        for a in (doc_starts, log_decay, out_grad, out_proj, query_rows, key_rows, value_rows)
    ))
    return pl.pallas_call(
        finish,
        out_shape=(result, result, result),
        in_specs=[pl.BlockSpec(memory_space=pltpu.VMEM)] * 6 + [any_space],
        out_specs=(any_space,) * 3,
        scratch_shapes=[
            pltpu.VMEM((tokens, width), F32),
            pltpu.VMEM((tokens, width), F32),
            pltpu.SemaphoreType.DMA((3, 4)),
        ],
        compiler_params=pltpu.CompilerParams(vmem_limit_bytes=16 * 1024 * 1024),
        name="finish",
    )(adjoint, outflow, key_rows, value_rows, k_part, v_part, q_part)


def solution(mesh):
    lines = PLANE
    planes = mesh.shape["ctx"] // (2 * lines)
    return jax.shard_map(
        functools.partial(on_device, planes, lines),
        mesh=mesh,
        in_specs=(
            P("ctx", "head"),
            P("head", None),
            P("ctx", "head"),
            P("ctx", "head"),
            P("ctx", "head"),
            P("head", "ctx"),
            P(),
        ),
        out_specs=(P("ctx", "head"), P("ctx", "head"), P("ctx", "head")),
        check_vma=False,
    )
```

```python
import functools

import jax
import jax.numpy as jnp
from jax import lax
from jax.experimental import pallas as pl
from jax.experimental.pallas import tpu as pltpu
from jax.sharding import PartitionSpec as P

PLANE = 4
CHUNKS = 4
MESH = pl.DeviceIdType.MESH
F32 = jnp.float32
BF16 = jnp.bfloat16


def nn(a, b):
    return lax.dot_general(a, b, (((1,), (0,)), ((), ())), preferred_element_type=F32)


def nt(a, b):
    return lax.dot_general(a, b, (((1,), (1,)), ((), ())), preferred_element_type=F32)


def tn(a, b):
    return lax.dot_general(a, b, (((0,), (0,)), ((), ())), preferred_element_type=F32)


def far_first(n, size):
    half = size // 2
    return half + lax.rem(n + 1, 2) * (n // 2) - lax.rem(n, 2) * ((n + 1) // 2)


def ring_offsets(distance, size):
    return sorted({distance % size, -distance % size} - {0})


def kernel(
    planes, lines,
    doc_in, ld_in, og, w, q, k, v,
    qg, kg, vg, adjoint, outflow, k_out, v_out,
    doc, ld, og_v, w_v, q_v, k_v, v_v, acc, g_v, wt, sm, fm, dq, inc, outc, qg_v, kg_v, vg_v, oc_v,
    t_send, t_other, tc_send, t_rec, own, core_send, core_rec, ch_send, ch_rec, en_send, en_rec,
    back_send, back_rec, state,
    local_sem, out_sem, y_send, y_rec, t_sem, c_send, c_rec, greet_sem,
):
    tokens, width = q_v.shape
    feats = og_v.shape[2]
    size = width // 2
    chips, height, wide = ch_send.shape[1:]
    chunk = tokens // CHUNKS
    factor = size ** -0.5
    ctx, y = lax.axis_index("ctx"), lax.axis_index("head")
    chip, core = ctx // 2, ctx % 2
    z, x = chip // lines, chip % lines
    first_core = core == 0
    other = chip * 2 + 1 - core
    right, left = (y + 1) % 4, (y + 3) % 4
    owners = (y, left, right, (y + 2) % 4)

    def at_chip(dz, dx):
        return (((z + dz) % planes * lines + (x + dx) % lines) * 2 + core, y)

    near_z, far_z = ring_offsets(1, planes), ring_offsets(2, planes)
    near_x = [at_chip(0, d) for d in ring_offsets(1, lines)]
    near_z, far_z = [at_chip(d, 0) for d in near_z], [at_chip(d, 0) for d in far_z]
    rounds = [near_z + near_x, near_z + far_z, far_z]
    barrier = pltpu.get_barrier_semaphore()
    entry = [(ctx, left), (ctx, right), (other, y)] + near_z + near_x
    for near in entry:
        pl.semaphore_signal(barrier, inc=1, device_id=near, device_id_type=MESH)
    loads = [pltpu.make_async_copy(og, og_v.at[0], local_sem.at[0])]
    for i, (src, dst) in enumerate(((k, k_v), (v, v_v), (q, q_v))):
        loads.append(pltpu.make_async_copy(src, dst, local_sem.at[1 + i]))
    for i in range(4):
        start = pl.multiple_of(owners[i] * feats, 128)
        loads.append(pltpu.make_async_copy(w.at[:, pl.ds(start, feats)], w_v.at[i], local_sem.at[4 + i]))
    small = [pltpu.make_async_copy(ld_in, ld, local_sem.at[8]), pltpu.make_async_copy(doc_in, doc, local_sem.at[9])]
    for load in small + loads:
        load.start()
    pl.semaphore_wait(barrier, len(entry))

    def tell(i):
        for to in rounds[i]:
            pl.semaphore_signal(greet_sem.at[i], inc=1, device_id=to, device_id_type=MESH)

    def hear(i):
        if rounds[i]:
            pl.semaphore_wait(greet_sem.at[i], len(rounds[i]))

    def hop(src_slot, dst_slot, c, to, lane):
        at = pl.ds(c * chunk, chunk)
        return pltpu.make_async_remote_copy(
            src_ref=og_v.at[src_slot, at], dst_ref=og_v.at[dst_slot, at],
            send_sem=y_send.at[lane, c], recv_sem=y_rec.at[dst_slot - 1, c],
            device_id=(ctx, to), device_id_type=MESH,
        )

    to_right = [hop(0, 1, c, right, 0) for c in range(CHUNKS)]
    to_left = [hop(0, 2, c, left, 1) for c in range(CHUNKS)]
    onward = [hop(1, 3, c, right, 2) if c < CHUNKS // 2 else hop(2, 3, c, left, 2) for c in range(CHUNKS)]
    loads[0].wait()
    for c in range(CHUNKS):
        to_right[c].start()
        to_left[CHUNKS - 1 - c].start()
    tell(0)

    offset = ctx * tokens
    lane = lax.broadcasted_iota(jnp.int32, (8, tokens), 1)
    for load in small:
        load.wait()
    docs = [doc[i] for i in range(doc.shape[0])]

    def segment(places):
        total = jnp.zeros(places.shape, jnp.int32)
        for d in docs:
            total = total + (d <= places).astype(jnp.int32)
        return total

    def segment_at(place):
        total = jnp.int32(0)
        for d in docs:
            total = total + (d <= place).astype(jnp.int32)
        return total

    before, last = segment_at(offset - 1), segment_at(offset + tokens - 1)
    seg_row = segment(offset + lane)[0:1]
    row_at = lax.broadcasted_iota(jnp.int32, (tokens, tokens), 0)
    col_at = lax.broadcasted_iota(jnp.int32, (tokens, tokens), 1)
    seg_col = segment(offset + lax.broadcasted_iota(jnp.int32, (tokens, 1), 0))
    in_col = (seg_col == before).astype(F32)
    out_col = (seg_col == last).astype(F32)
    same = (seg_col == seg_row) & (col_at <= row_at)
    cums = []
    for h in range(2):
        cum = jnp.broadcast_to(ld[h : h + 1, :], (8, tokens))
        step = 1
        while step < tokens:
            cum = cum + jnp.where(lane >= step, pltpu.roll(cum, step, 1), 0.0)
            step *= 2
        whole = jnp.sum(jnp.where(lane == tokens - 1, cum, 0.0), axis=1, keepdims=True)
        through = jnp.exp(whole) * jnp.where(before == last, 1.0, 0.0)
        t_send[h] = jnp.broadcast_to(through, (8, t_send.shape[2]))
        cum_row = cum[0:1]
        cum_col = jnp.sum(jnp.where(row_at == col_at, cum_row, 0.0), axis=1, keepdims=True)
        inc[h] = jnp.exp(cum_col) * in_col
        outc[h] = jnp.exp(whole[0:1] - cum_col) * out_col
        cums.append((cum_row, cum_col))

    def to_core(src, dst, send, recv):
        return pltpu.make_async_remote_copy(
            src_ref=src, dst_ref=dst, send_sem=send, recv_sem=recv,
            device_id=(other, y), device_id_type=MESH,
        )

    columns = sorted(range(lines), key=lambda d: -min(d, lines - d))
    columns = [(x + d) % lines for d in columns]

    def to_chips(src, dst, send, recv, index):
        def one(j):
            pltpu.make_async_remote_copy(
                src_ref=src.at[index(j)], dst_ref=dst.at[chip], send_sem=send, recv_sem=recv,
                device_id=(j * 2 + core, y), device_id_type=MESH,
            ).start()

        def row(n, c):
            there = (z + far_first(n, planes)) % planes * lines
            for line in columns[:-1]:
                one(there + line)

            @pl.when(n < planes - 1)
            def _():
                one(there + columns[-1])

            return c

        lax.fori_loop(0, planes, row, 0)

    def arrived(ref, count, sem):
        part = ref.at[pl.ds(0, count)]
        pltpu.make_async_copy(part, part, sem).wait()

    t_copy = to_core(t_send.at[1 - core], t_other, t_sem.at[0], t_sem.at[1])
    t_copy.start()

    def decay(ref):
        return ref[0:1, 0:1]

    def core_copy(direction):
        return to_core(
            core_send.at[direction], core_rec.at[direction], c_send.at[direction, 0], c_rec.at[direction, 0]
        )

    def back_copy(direction):
        return to_core(
            back_send.at[direction], adjoint if direction else back_rec, c_send.at[direction, 3], c_rec.at[direction, 3]
        )

    def first_send(direction):
        core_send[direction] = own[direction, 1 - core].astype(BF16)
        core_copy(direction).start()

    def pieces(ref, direction, whole):
        half = chips // 2 if chips > 1 else 1
        for i in range(2):
            part = whole[:, i * wide : (i + 1) * wide]
            ref[direction, i * half : (i + 1) * half] = part.reshape(half, height, wide)

    def second_send(direction):
        core_copy(direction).wait_recv()
        mine, theirs = own[direction, core], core_rec[direction].astype(F32)
        earlier = first_core if direction == 0 else jnp.logical_not(first_core)
        a = jnp.where(earlier, decay(t_other), 1.0)
        b = jnp.where(earlier, 1.0, decay(t_send.at[core]))
        pieces(ch_send, direction, (a * mine + b * theirs).astype(BF16))
        to_chips(
            ch_send.at[direction], ch_rec.at[direction], c_send.at[direction, 1], c_rec.at[direction, 1],
            lambda j: j,
        )
        ch_rec[direction, chip] = ch_send[direction, chip]

    def third_send(direction):
        arrived(ch_rec.at[direction], chips - 1, c_rec.at[direction, 1])
        run = jnp.zeros((height // 8, 8, wide), F32)
        for i in range(chips) if direction == 0 else reversed(range(chips)):
            en_send[direction, i] = run.reshape(height, wide).astype(BF16)
            here = ch_rec[direction, i].astype(F32).reshape(height // 8, 8, wide)
            run = t_rec[i, :, 0:wide] * run + here
        to_chips(
            en_send.at[direction], en_rec.at[direction], c_send.at[direction, 2], c_rec.at[direction, 2],
            lambda j: j,
        )
        en_rec[direction, chip] = en_send[direction, chip]

    def fourth_send(direction):
        arrived(en_rec.at[direction], chips - 1, c_rec.at[direction, 2])
        half = chips // 2
        parts = [en_rec[direction, i * half : (i + 1) * half].reshape(size, wide) for i in range(2)]
        entering = jnp.concatenate(parts, axis=1).astype(F32)
        earlier = first_core if direction == 0 else jnp.logical_not(first_core)
        a = jnp.where(earlier, decay(t_send.at[core]), 1.0)
        b = jnp.where(earlier, 1.0, 0.0)
        back_send[direction] = (a * entering + b * own[direction, core]).astype(BF16)
        back_copy(direction).start()
        a = jnp.where(earlier, 1.0, decay(t_other))
        return (a * entering + (1.0 - b) * core_rec[direction].astype(F32)).astype(BF16)

    def cols(h):
        return slice(h * size, (h + 1) * size)

    loads[1].wait()
    loads[2].wait()
    for h in range(2):
        decayed = (k_v[:, cols(h)].astype(F32) * outc[h]).astype(BF16)
        own[0, h] = tn(decayed, v_v[:, cols(h)])
    first_send(0)
    hear(0)
    tell(1)

    loads[3].wait()
    q_v[...] = q_v[...] * jnp.asarray(factor, BF16)
    at_lane = lax.broadcasted_iota(jnp.int32, oc_v.shape, 1)
    oc_v[...] = jnp.where(at_lane == 0, outc[0], outc[1])
    for h in range(2):
        dq[:, cols(h)] = (q_v[:, cols(h)].astype(F32) * inc[h]).astype(BF16)
        cum_row, cum_col = cums[h]
        wt[h] = jnp.exp(jnp.where(same, cum_col - cum_row, -1e30))
        sm[h] = (nt(q_v[:, cols(h)], k_v[:, cols(h)]) * wt[h]).astype(BF16)
    hear(1)
    tell(2)
    loads[4].wait()
    acc[...] = nt(og_v[0], w_v[0])
    for i in range(1, 4):
        loads[4 + i].wait()
    hear(2)
    t_copy.wait_recv()
    tc_send[...] = t_send[core] * t_other[...]
    to_chips(tc_send, t_rec, t_sem.at[2], t_sem.at[3], lambda j: slice(None))
    t_rec[chip] = tc_send[...]
    second_send(0)

    def add(slot, c):
        at = slice(c * chunk, (c + 1) * chunk)
        acc[at, :] += nt(og_v[slot, at], w_v[slot])

    half = CHUNKS // 2
    for c in range(half):
        to_right[c].wait_recv()
        onward[c].start()
        to_left[CHUNKS - 1 - c].wait_recv()
        onward[CHUNKS - 1 - c].start()
        add(1, c)
        add(2, CHUNKS - 1 - c)
    for c in range(half):
        to_right[half + c].wait_recv()
        add(1, half + c)
        to_left[half - 1 - c].wait_recv()
        add(2, half - 1 - c)

    heads = (1 - core, core)
    for h in range(2):
        own[1, h] = jnp.zeros((size, size), F32)
    for c in range(half):
        for at in (c, CHUNKS - 1 - c):
            onward[at].wait_recv()
            span = slice(at * chunk, (at + 1) * chunk)
            g_v[span, :] = (acc[span, :] + nt(og_v[3, span], w_v[3])).astype(BF16)
        for i in range(2):
            at = pl.ds(pl.multiple_of(heads[i] * size, 128), size)
            total = own[1, heads[i]]
            for r in (c, CHUNKS - 1 - c):
                span = slice(r * chunk, (r + 1) * chunk)
                total = total + tn(dq[span, at], g_v[span, at])
            own[1, heads[i]] = total
            if c == half - 1 and i == 0:
                first_send(1)

    outs = [pltpu.make_async_copy(oc_v, outflow, out_sem.at[3, 0])]
    for i, (src, dst) in enumerate(((k_v, k_out), (v_v, v_out))):
        outs.append(pltpu.make_async_copy(src, dst, out_sem.at[4, i]))
    for copy in outs:
        copy.start()

    def put(src, dst, h, i):
        copy = pltpu.make_async_copy(src.at[:, cols(h)], dst.at[:, cols(h)], out_sem.at[i, h])
        copy.start()
        outs.append(copy)

    for h in range(2):
        fm[h] = (nt(g_v[:, cols(h)], v_v[:, cols(h)]) * wt[h]).astype(BF16)
    second_send(1)
    arrived(t_rec, chips - 1, t_sem.at[3])
    third_send(0)
    for h in range(2):
        kg_v[:, cols(h)] = tn(fm[h], q_v[:, cols(h)])
        vg_v[:, cols(h)] = tn(sm[h], g_v[:, cols(h)])
    third_send(1)
    state[core] = fourth_send(0)
    back_copy(0).wait_recv()
    state[1 - core] = back_rec[...]
    for h in range(2):
        entering = nt(g_v[:, cols(h)], state[h])
        qg_v[:, cols(h)] = factor * (nn(fm[h], k_v[:, cols(h)]) + inc[h] * entering)
        put(qg_v, qg, h, 0)

    for copy in to_right + to_left + onward + [t_copy]:
        copy.wait_send()
    arrived(t_rec, chips - 1, t_sem.at[2])
    for direction in range(2):
        core_copy(direction).wait_send()
        arrived(ch_send.at[direction], chips - 1, c_send.at[direction, 1])
    arrived(en_send.at[0], chips - 1, c_send.at[0, 2])
    back_copy(0).wait_send()

    mine, theirs = pl.ds(pl.multiple_of(core * size, 128), size), pl.ds(pl.multiple_of(size - core * size, 128), size)
    for i, (src, dst) in enumerate(((kg_v, kg), (vg_v, vg))):
        outs.append(pltpu.make_async_copy(src.at[:, theirs], dst.at[:, theirs], out_sem.at[1 + i, 0]))
        outs[-1].start()
    entering = fourth_send(1)
    kg_v[:, mine] += outc[core] * nt(v_v[:, mine], entering)
    vg_v[:, mine] += outc[core] * nn(k_v[:, mine], entering)
    for i, (src, dst) in enumerate(((kg_v, kg), (vg_v, vg))):
        outs.append(pltpu.make_async_copy(src.at[:, mine], dst.at[:, mine], out_sem.at[1 + i, 1]))
        outs[-1].start()
    arrived(en_send.at[1], chips - 1, c_send.at[1, 2])
    for copy in outs:
        copy.wait()
    back_copy(1).wait()


def finish(adjoint, outflow, k, v, k_part, v_part, q_part, qg, kg, vg, k_all, v_all, sem):
    tokens, width = k.shape
    size = width // 2
    step = tokens // 4
    core = lax.axis_index("ctx") % 2
    done, left = pl.ds(pl.multiple_of(core * size, 128), size), pl.ds(pl.multiple_of(size - core * size, 128), size)
    outs = [
        pltpu.make_async_copy(q_part, qg, sem.at[2, 0]),
        pltpu.make_async_copy(k_part.at[:, done], kg.at[:, done], sem.at[2, 1]),
        pltpu.make_async_copy(v_part.at[:, done], vg.at[:, done], sem.at[2, 2]),
    ]
    for copy in outs:
        copy.start()
    for c in range(4):
        at = slice(c * step, (c + 1) * step)
        rows = pl.ds(c * step, step)
        flow = jnp.where(core == 0, outflow[at, 1:2], outflow[at, 0:1])
        for i, (part, whole, out) in enumerate(((k_part, k_all, kg), (v_part, v_all, vg))):
            term = nn(k[at, left], adjoint[...]) if i else nt(v[at, left], adjoint[...])
            whole[at, :] = part[at, left] + flow * term
            copy = pltpu.make_async_copy(whole.at[rows], out.at[rows, left], sem.at[i, c])
            copy.start()
            outs.append(copy)
    for copy in outs:
        copy.wait()


def on_device(planes, lines, out_grad, out_proj, query_rows, key_rows, value_rows, log_decay, doc_starts):
    tokens, width = query_rows.shape
    feats = out_grad.shape[1]
    size = width // 2
    chips = planes * lines
    height, wide = size * 2 // chips, size // 2
    any_space = pl.BlockSpec(memory_space=pl.ANY)
    result = jax.ShapeDtypeStruct((tokens, width), F32)
    adjoint = jax.ShapeDtypeStruct((size, size), BF16)
    outflow = jax.ShapeDtypeStruct((tokens, 128), F32)
    tile = (8, 128)
    scratch = [
        pltpu.SMEM(doc_starts.shape, doc_starts.dtype),
        pltpu.VMEM(log_decay.shape, F32),
        pltpu.VMEM((4, tokens, feats), BF16),
        pltpu.VMEM((4, width, feats), BF16),
        pltpu.VMEM((tokens, width), BF16),
        pltpu.VMEM((tokens, width), BF16),
        pltpu.VMEM((tokens, width), BF16),
        pltpu.VMEM((tokens, width), F32),
        pltpu.VMEM((tokens, width), BF16),
        pltpu.VMEM((2, tokens, tokens), F32),
        pltpu.VMEM((2, tokens, tokens), BF16),
        pltpu.VMEM((2, tokens, tokens), BF16),
        pltpu.VMEM((tokens, width), BF16),
        pltpu.VMEM((2, tokens, 1), F32),
        pltpu.VMEM((2, tokens, 1), F32),
        pltpu.VMEM((tokens, width), F32),
        pltpu.VMEM((tokens, width), F32),
        pltpu.VMEM((tokens, width), F32),
        pltpu.VMEM((tokens, 128), F32),
        pltpu.VMEM((2,) + tile, F32),
        pltpu.VMEM(tile, F32),
        pltpu.VMEM(tile, F32),
        pltpu.VMEM((chips,) + tile, F32),
        pltpu.VMEM((2, 2, size, size), F32),
        pltpu.VMEM((2, size, size), BF16),
        pltpu.VMEM((2, size, size), BF16),
        pltpu.VMEM((2, chips, height, wide), BF16),
        pltpu.VMEM((2, chips, height, wide), BF16),
        pltpu.VMEM((2, chips, height, wide), BF16),
        pltpu.VMEM((2, chips, height, wide), BF16),
        pltpu.VMEM((2, size, size), BF16),
        pltpu.VMEM((size, size), BF16),
        pltpu.VMEM((2, size, size), BF16),
        pltpu.SemaphoreType.DMA((10,)),
        pltpu.SemaphoreType.DMA((5, 2)),
        pltpu.SemaphoreType.DMA((3, CHUNKS)),
        pltpu.SemaphoreType.DMA((3, CHUNKS)),
        pltpu.SemaphoreType.DMA((4,)),
        pltpu.SemaphoreType.DMA((2, 4)),
        pltpu.SemaphoreType.DMA((2, 4)),
        pltpu.SemaphoreType.REGULAR((3,)),
    ]
    q_part, k_part, v_part, adjoint, outflow, key_rows, value_rows = pl.pallas_call(
        functools.partial(kernel, planes, lines),
        out_shape=tuple(pltpu.VMEM(a.shape, a.dtype) for a in (result, result, result, adjoint, outflow, key_rows, value_rows)),
        in_specs=[any_space] * 7,
        out_specs=(any_space,) * 7,
        scratch_shapes=scratch,
        compiler_params=pltpu.CompilerParams(
            collective_id=0, has_side_effects=True, vmem_limit_bytes=32 * 1024 * 1024
        ),
        name="retention_backward",
    )(*(
        pltpu.with_memory_space_constraint(a, pltpu.HBM)
        for a in (doc_starts, log_decay, out_grad, out_proj, query_rows, key_rows, value_rows)
    ))
    return pl.pallas_call(
        finish,
        out_shape=(result, result, result),
        in_specs=[pl.BlockSpec(memory_space=pltpu.VMEM)] * 6 + [any_space],
        out_specs=(any_space,) * 3,
        scratch_shapes=[
            pltpu.VMEM((tokens, size), F32),
            pltpu.VMEM((tokens, size), F32),
            pltpu.SemaphoreType.DMA((3, 4)),
        ],
        compiler_params=pltpu.CompilerParams(vmem_limit_bytes=16 * 1024 * 1024),
        name="finish",
    )(adjoint, outflow, key_rows, value_rows, k_part, v_part, q_part)


def solution(mesh):
    lines = PLANE
    planes = mesh.shape["ctx"] // (2 * lines)
    return jax.shard_map(
        functools.partial(on_device, planes, lines),
        mesh=mesh,
        in_specs=(
            P("ctx", "head"),
            P("head", None),
            P("ctx", "head"),
            P("ctx", "head"),
            P("ctx", "head"),
            P("head", "ctx"),
            P(),
        ),
        out_specs=(P("ctx", "head"), P("ctx", "head"), P("ctx", "head")),
        check_vma=False,
    )
```

```python
import functools

import jax
import jax.numpy as jnp
from jax import lax
from jax.experimental import pallas as pl
from jax.experimental.pallas import tpu as pltpu
from jax.sharding import PartitionSpec as P

PLANE = 4
CHUNKS = 4
MESH = pl.DeviceIdType.MESH
F32 = jnp.float32
BF16 = jnp.bfloat16


def nn(a, b):
    return lax.dot_general(a, b, (((1,), (0,)), ((), ())), preferred_element_type=F32)


def nt(a, b):
    return lax.dot_general(a, b, (((1,), (1,)), ((), ())), preferred_element_type=F32)


def tn(a, b):
    return lax.dot_general(a, b, (((0,), (0,)), ((), ())), preferred_element_type=F32)


def far_first(n, size):
    half = size // 2
    return half + lax.rem(n + 1, 2) * (n // 2) - lax.rem(n, 2) * ((n + 1) // 2)


def ring_offsets(distance, size):
    return sorted({distance % size, -distance % size} - {0})


def kernel(
    planes, lines,
    doc_in, ld_in, og, w, q, k, v,
    qg, kg, vg, adjoint, outflow, k_out, v_out,
    doc, ld, og_v, w_v, w_t, q_v, k_v, v_v, acc, g_v, wt, sm, fm, dq, inc, outc, qg_v, kg_v, vg_v, oc_v,
    t_send, t_other, tc_send, t_rec, own, core_send, core_rec, ch_send, ch_rec, en_send, en_rec,
    back_send, back_rec, state,
    local_sem, out_sem, y_send, y_rec, t_sem, c_send, c_rec, greet_sem,
):
    tokens, width = q_v.shape
    feats = og_v.shape[2]
    size = width // 2
    chips, height, wide = ch_send.shape[1:]
    chunk = tokens // CHUNKS
    factor = size ** -0.5
    ctx, y = lax.axis_index("ctx"), lax.axis_index("head")
    chip, core = ctx // 2, ctx % 2
    z, x = chip // lines, chip % lines
    first_core = core == 0
    other = chip * 2 + 1 - core
    right, left = (y + 1) % 4, (y + 3) % 4
    owners = (y, left, right, (y + 2) % 4)

    def at_chip(dz, dx):
        return (((z + dz) % planes * lines + (x + dx) % lines) * 2 + core, y)

    near_z, far_z = ring_offsets(1, planes), ring_offsets(2, planes)
    near_x = [at_chip(0, d) for d in ring_offsets(1, lines)]
    near_z, far_z = [at_chip(d, 0) for d in near_z], [at_chip(d, 0) for d in far_z]
    rounds = [near_z + near_x, near_z + far_z, far_z]
    barrier = pltpu.get_barrier_semaphore()
    entry = [(ctx, left), (ctx, right), (other, y)] + near_z + near_x
    for near in entry:
        pl.semaphore_signal(barrier, inc=1, device_id=near, device_id_type=MESH)
    loads = [pltpu.make_async_copy(og, og_v.at[0], local_sem.at[0])]
    for i, (src, dst) in enumerate(((k, k_v), (v, v_v), (q, q_v))):
        loads.append(pltpu.make_async_copy(src, dst, local_sem.at[1 + i]))
    for i in range(4):
        start = pl.multiple_of(owners[i] * feats, 128)
        loads.append(pltpu.make_async_copy(w.at[:, pl.ds(start, feats)], w_v.at[i], local_sem.at[4 + i]))
    small = [pltpu.make_async_copy(ld_in, ld, local_sem.at[8]), pltpu.make_async_copy(doc_in, doc, local_sem.at[9])]
    for load in small + loads:
        load.start()
    pl.semaphore_wait(barrier, len(entry))

    def tell(i):
        for to in rounds[i]:
            pl.semaphore_signal(greet_sem.at[i], inc=1, device_id=to, device_id_type=MESH)

    def hear(i):
        if rounds[i]:
            pl.semaphore_wait(greet_sem.at[i], len(rounds[i]))

    def hop(src_slot, dst_slot, c, to, lane):
        at = pl.ds(c * chunk, chunk)
        return pltpu.make_async_remote_copy(
            src_ref=og_v.at[src_slot, at], dst_ref=og_v.at[dst_slot, at],
            send_sem=y_send.at[lane, c], recv_sem=y_rec.at[dst_slot - 1, c],
            device_id=(ctx, to), device_id_type=MESH,
        )

    to_right = [hop(0, 1, c, right, 0) for c in range(CHUNKS)]
    to_left = [hop(0, 2, c, left, 1) for c in range(CHUNKS)]
    onward = [hop(1, 3, c, right, 2) if c < CHUNKS // 2 else hop(2, 3, c, left, 2) for c in range(CHUNKS)]
    loads[0].wait()
    for c in range(CHUNKS):
        to_right[c].start()
        to_left[CHUNKS - 1 - c].start()
    tell(0)

    offset = ctx * tokens
    lane = lax.broadcasted_iota(jnp.int32, (8, tokens), 1)
    for load in small:
        load.wait()
    docs = [doc[i] for i in range(doc.shape[0])]

    def segment(places):
        total = jnp.zeros(places.shape, jnp.int32)
        for d in docs:
            total = total + (d <= places).astype(jnp.int32)
        return total

    def segment_at(place):
        total = jnp.int32(0)
        for d in docs:
            total = total + (d <= place).astype(jnp.int32)
        return total

    before, last = segment_at(offset - 1), segment_at(offset + tokens - 1)
    seg_row = segment(offset + lane)[0:1]
    row_at = lax.broadcasted_iota(jnp.int32, (tokens, tokens), 0)
    col_at = lax.broadcasted_iota(jnp.int32, (tokens, tokens), 1)
    seg_col = segment(offset + lax.broadcasted_iota(jnp.int32, (tokens, 1), 0))
    in_col = (seg_col == before).astype(F32)
    out_col = (seg_col == last).astype(F32)
    same = (seg_col == seg_row) & (col_at <= row_at)
    cums = []
    for h in range(2):
        cum = jnp.broadcast_to(ld[h : h + 1, :], (8, tokens))
        step = 1
        while step < tokens:
            cum = cum + jnp.where(lane >= step, pltpu.roll(cum, step, 1), 0.0)
            step *= 2
        whole = jnp.sum(jnp.where(lane == tokens - 1, cum, 0.0), axis=1, keepdims=True)
        through = jnp.exp(whole) * jnp.where(before == last, 1.0, 0.0)
        t_send[h] = jnp.broadcast_to(through, (8, t_send.shape[2]))
        cum_row = cum[0:1]
        cum_col = jnp.sum(jnp.where(row_at == col_at, cum_row, 0.0), axis=1, keepdims=True)
        inc[h] = jnp.exp(cum_col) * in_col
        outc[h] = jnp.exp(whole[0:1] - cum_col) * out_col
        cums.append((cum_row, cum_col))

    def to_core(src, dst, send, recv):
        return pltpu.make_async_remote_copy(
            src_ref=src, dst_ref=dst, send_sem=send, recv_sem=recv,
            device_id=(other, y), device_id_type=MESH,
        )

    columns = sorted(range(lines), key=lambda d: -min(d, lines - d))
    columns = [(x + d) % lines for d in columns]

    def to_chips(src, dst, send, recv, index):
        def one(j):
            pltpu.make_async_remote_copy(
                src_ref=src.at[index(j)], dst_ref=dst.at[chip], send_sem=send, recv_sem=recv,
                device_id=(j * 2 + core, y), device_id_type=MESH,
            ).start()

        def row(n, c):
            there = (z + far_first(n, planes)) % planes * lines
            for line in columns[:-1]:
                one(there + line)

            @pl.when(n < planes - 1)
            def _():
                one(there + columns[-1])

            return c

        lax.fori_loop(0, planes, row, 0)

    def arrived(ref, count, sem):
        part = ref.at[pl.ds(0, count)]
        pltpu.make_async_copy(part, part, sem).wait()

    t_copy = to_core(t_send.at[1 - core], t_other, t_sem.at[0], t_sem.at[1])
    t_copy.start()

    def decay(ref):
        return ref[0:1, 0:1]

    def core_copy(direction):
        return to_core(
            core_send.at[direction], core_rec.at[direction], c_send.at[direction, 0], c_rec.at[direction, 0]
        )

    def back_copy(direction):
        return to_core(
            back_send.at[direction], adjoint if direction else back_rec, c_send.at[direction, 3], c_rec.at[direction, 3]
        )

    def first_send(direction):
        core_send[direction] = own[direction, 1 - core].astype(BF16)
        core_copy(direction).start()

    def pieces(ref, direction, whole):
        half = chips // 2 if chips > 1 else 1
        for i in range(2):
            part = whole[:, i * wide : (i + 1) * wide]
            ref[direction, i * half : (i + 1) * half] = part.reshape(half, height, wide)

    def second_send(direction):
        core_copy(direction).wait_recv()
        mine, theirs = own[direction, core], core_rec[direction].astype(F32)
        earlier = first_core if direction == 0 else jnp.logical_not(first_core)
        a = jnp.where(earlier, decay(t_other), 1.0)
        b = jnp.where(earlier, 1.0, decay(t_send.at[core]))
        pieces(ch_send, direction, (a * mine + b * theirs).astype(BF16))
        to_chips(
            ch_send.at[direction], ch_rec.at[direction], c_send.at[direction, 1], c_rec.at[direction, 1],
            lambda j: j,
        )
        ch_rec[direction, chip] = ch_send[direction, chip]

    def third_send(direction):
        arrived(ch_rec.at[direction], chips - 1, c_rec.at[direction, 1])
        run = jnp.zeros((height // 8, 8, wide), F32)
        for i in range(chips) if direction == 0 else reversed(range(chips)):
            en_send[direction, i] = run.reshape(height, wide).astype(BF16)
            here = ch_rec[direction, i].astype(F32).reshape(height // 8, 8, wide)
            run = t_rec[i, :, 0:wide] * run + here
        to_chips(
            en_send.at[direction], en_rec.at[direction], c_send.at[direction, 2], c_rec.at[direction, 2],
            lambda j: j,
        )
        en_rec[direction, chip] = en_send[direction, chip]

    def fourth_send(direction):
        arrived(en_rec.at[direction], chips - 1, c_rec.at[direction, 2])
        half = chips // 2
        parts = [en_rec[direction, i * half : (i + 1) * half].reshape(size, wide) for i in range(2)]
        entering = jnp.concatenate(parts, axis=1).astype(F32)
        earlier = first_core if direction == 0 else jnp.logical_not(first_core)
        a = jnp.where(earlier, decay(t_send.at[core]), 1.0)
        b = jnp.where(earlier, 1.0, 0.0)
        back_send[direction] = (a * entering + b * own[direction, core]).astype(BF16)
        back_copy(direction).start()
        a = jnp.where(earlier, 1.0, decay(t_other))
        return (a * entering + (1.0 - b) * core_rec[direction].astype(F32)).astype(BF16)

    def cols(h):
        return slice(h * size, (h + 1) * size)

    loads[1].wait()
    loads[2].wait()
    for h in range(2):
        decayed = (k_v[:, cols(h)].astype(F32) * outc[h]).astype(BF16)
        own[0, h] = tn(decayed, v_v[:, cols(h)])
    first_send(0)
    hear(0)
    tell(1)

    loads[3].wait()
    q_v[...] = q_v[...] * jnp.asarray(factor, BF16)
    at_lane = lax.broadcasted_iota(jnp.int32, oc_v.shape, 1)
    oc_v[...] = jnp.where(at_lane == 0, outc[0], outc[1])
    for h in range(2):
        dq[h] = (q_v[:, cols(h)].astype(F32) * inc[h]).astype(BF16).T
        cum_row, cum_col = cums[h]
        wt[h] = jnp.exp(jnp.where(same, cum_col - cum_row, -1e30))
        sm[h] = (nt(q_v[:, cols(h)], k_v[:, cols(h)]) * wt[h]).astype(BF16)
    hear(1)
    tell(2)
    loads[4].wait()
    acc[...] = nt(og_v[0], w_v[0])
    for i in range(1, 4):
        loads[4 + i].wait()
        w_t[i - 1] = w_v[i].T
    hear(2)
    t_copy.wait_recv()
    tc_send[...] = t_send[core] * t_other[...]
    to_chips(tc_send, t_rec, t_sem.at[2], t_sem.at[3], lambda j: slice(None))
    t_rec[chip] = tc_send[...]
    second_send(0)

    def add(slot, c):
        at = slice(c * chunk, (c + 1) * chunk)
        acc[at, :] += nn(og_v[slot, at], w_t[slot - 1])

    half = CHUNKS // 2
    for c in range(half):
        to_right[c].wait_recv()
        onward[c].start()
        to_left[CHUNKS - 1 - c].wait_recv()
        onward[CHUNKS - 1 - c].start()
        add(1, c)
        add(2, CHUNKS - 1 - c)
    for c in range(half):
        to_right[half + c].wait_recv()
        add(1, half + c)
        to_left[half - 1 - c].wait_recv()
        add(2, half - 1 - c)

    heads = (1 - core, core)
    for h in range(2):
        own[1, h] = jnp.zeros((size, size), F32)
    for c in range(half):
        for at in (c, CHUNKS - 1 - c):
            onward[at].wait_recv()
            span = slice(at * chunk, (at + 1) * chunk)
            g_v[span, :] = (acc[span, :] + nn(og_v[3, span], w_t[2])).astype(BF16)
        for i in range(2):
            at = pl.ds(pl.multiple_of(heads[i] * size, 128), size)
            total = own[1, heads[i]]
            for r in (c, CHUNKS - 1 - c):
                span = slice(r * chunk, (r + 1) * chunk)
                total = total + nn(dq[heads[i], :, span], g_v[span, at])
            own[1, heads[i]] = total
            if c == half - 1 and i == 0:
                first_send(1)

    outs = [pltpu.make_async_copy(oc_v, outflow, out_sem.at[3, 0])]
    for i, (src, dst) in enumerate(((k_v, k_out), (v_v, v_out))):
        outs.append(pltpu.make_async_copy(src, dst, out_sem.at[4, i]))
    for copy in outs:
        copy.start()

    def put(src, dst, h, i):
        copy = pltpu.make_async_copy(src.at[:, cols(h)], dst.at[:, cols(h)], out_sem.at[i, h])
        copy.start()
        outs.append(copy)

    second_send(1)
    for h in range(2):
        fm[h] = (nt(g_v[:, cols(h)], v_v[:, cols(h)]) * wt[h]).astype(BF16)
    arrived(t_rec, chips - 1, t_sem.at[3])
    third_send(0)
    for h in range(2):
        kg_v[:, cols(h)] = tn(fm[h], q_v[:, cols(h)])
        vg_v[:, cols(h)] = tn(sm[h], g_v[:, cols(h)])
    third_send(1)
    state[core] = fourth_send(0)
    back_copy(0).wait_recv()
    state[1 - core] = back_rec[...]
    for h in range(2):
        entering = nt(g_v[:, cols(h)], state[h])
        qg_v[:, cols(h)] = factor * (nn(fm[h], k_v[:, cols(h)]) + inc[h] * entering)
        put(qg_v, qg, h, 0)

    for copy in to_right + to_left + onward + [t_copy]:
        copy.wait_send()
    arrived(t_rec, chips - 1, t_sem.at[2])
    for direction in range(2):
        core_copy(direction).wait_send()
        arrived(ch_send.at[direction], chips - 1, c_send.at[direction, 1])
    arrived(en_send.at[0], chips - 1, c_send.at[0, 2])
    back_copy(0).wait_send()

    mine, theirs = pl.ds(pl.multiple_of(core * size, 128), size), pl.ds(pl.multiple_of(size - core * size, 128), size)
    for i, (src, dst) in enumerate(((kg_v, kg), (vg_v, vg))):
        outs.append(pltpu.make_async_copy(src.at[:, theirs], dst.at[:, theirs], out_sem.at[1 + i, 0]))
        outs[-1].start()
    entering = fourth_send(1)
    kg_v[:, mine] += outc[core] * nt(v_v[:, mine], entering)
    vg_v[:, mine] += outc[core] * nn(k_v[:, mine], entering)
    for i, (src, dst) in enumerate(((kg_v, kg), (vg_v, vg))):
        outs.append(pltpu.make_async_copy(src.at[:, mine], dst.at[:, mine], out_sem.at[1 + i, 1]))
        outs[-1].start()
    arrived(en_send.at[1], chips - 1, c_send.at[1, 2])
    for copy in outs:
        copy.wait()
    back_copy(1).wait()


def finish(adjoint, outflow, k, v, k_part, v_part, q_part, qg, kg, vg, k_all, v_all, sem):
    tokens, width = k.shape
    size = width // 2
    step = tokens // 2
    core = lax.axis_index("ctx") % 2
    done, left = pl.ds(pl.multiple_of(core * size, 128), size), pl.ds(pl.multiple_of(size - core * size, 128), size)
    outs = [
        pltpu.make_async_copy(q_part, qg, sem.at[2, 0]),
        pltpu.make_async_copy(k_part.at[:, done], kg.at[:, done], sem.at[2, 1]),
        pltpu.make_async_copy(v_part.at[:, done], vg.at[:, done], sem.at[2, 2]),
    ]
    for copy in outs:
        copy.start()
    for c in range(2):
        at = slice(c * step, (c + 1) * step)
        rows = pl.ds(c * step, step)
        flow = jnp.where(core == 0, outflow[at, 1:2], outflow[at, 0:1])
        for i, (part, whole, out) in enumerate(((k_part, k_all, kg), (v_part, v_all, vg))):
            term = nn(k[at, left], adjoint[...]) if i else nt(v[at, left], adjoint[...])
            whole[at, :] = part[at, left] + flow * term
            copy = pltpu.make_async_copy(whole.at[rows], out.at[rows, left], sem.at[i, c])
            copy.start()
            outs.append(copy)
    for copy in outs:
        copy.wait()


def on_device(planes, lines, out_grad, out_proj, query_rows, key_rows, value_rows, log_decay, doc_starts):
    tokens, width = query_rows.shape
    feats = out_grad.shape[1]
    size = width // 2
    chips = planes * lines
    height, wide = size * 2 // chips, size // 2
    any_space = pl.BlockSpec(memory_space=pl.ANY)
    result = jax.ShapeDtypeStruct((tokens, width), F32)
    adjoint = jax.ShapeDtypeStruct((size, size), BF16)
    outflow = jax.ShapeDtypeStruct((tokens, 128), F32)
    tile = (8, 128)
    scratch = [
        pltpu.SMEM(doc_starts.shape, doc_starts.dtype),
        pltpu.VMEM(log_decay.shape, F32),
        pltpu.VMEM((4, tokens, feats), BF16),
        pltpu.VMEM((4, width, feats), BF16),
        pltpu.VMEM((3, feats, width), BF16),
        pltpu.VMEM((tokens, width), BF16),
        pltpu.VMEM((tokens, width), BF16),
        pltpu.VMEM((tokens, width), BF16),
        pltpu.VMEM((tokens, width), F32),
        pltpu.VMEM((tokens, width), BF16),
        pltpu.VMEM((2, tokens, tokens), F32),
        pltpu.VMEM((2, tokens, tokens), BF16),
        pltpu.VMEM((2, tokens, tokens), BF16),
        pltpu.VMEM((2, size, tokens), BF16),
        pltpu.VMEM((2, tokens, 1), F32),
        pltpu.VMEM((2, tokens, 1), F32),
        pltpu.VMEM((tokens, width), F32),
        pltpu.VMEM((tokens, width), F32),
        pltpu.VMEM((tokens, width), F32),
        pltpu.VMEM((tokens, 128), F32),
        pltpu.VMEM((2,) + tile, F32),
        pltpu.VMEM(tile, F32),
        pltpu.VMEM(tile, F32),
        pltpu.VMEM((chips,) + tile, F32),
        pltpu.VMEM((2, 2, size, size), F32),
        pltpu.VMEM((2, size, size), BF16),
        pltpu.VMEM((2, size, size), BF16),
        pltpu.VMEM((2, chips, height, wide), BF16),
        pltpu.VMEM((2, chips, height, wide), BF16),
        pltpu.VMEM((2, chips, height, wide), BF16),
        pltpu.VMEM((2, chips, height, wide), BF16),
        pltpu.VMEM((2, size, size), BF16),
        pltpu.VMEM((size, size), BF16),
        pltpu.VMEM((2, size, size), BF16),
        pltpu.SemaphoreType.DMA((10,)),
        pltpu.SemaphoreType.DMA((5, 2)),
        pltpu.SemaphoreType.DMA((3, CHUNKS)),
        pltpu.SemaphoreType.DMA((3, CHUNKS)),
        pltpu.SemaphoreType.DMA((4,)),
        pltpu.SemaphoreType.DMA((2, 4)),
        pltpu.SemaphoreType.DMA((2, 4)),
        pltpu.SemaphoreType.REGULAR((3,)),
    ]
    q_part, k_part, v_part, adjoint, outflow, key_rows, value_rows = pl.pallas_call(
        functools.partial(kernel, planes, lines),
        out_shape=tuple(pltpu.VMEM(a.shape, a.dtype) for a in (result, result, result, adjoint, outflow, key_rows, value_rows)),
        in_specs=[any_space] * 7,
        out_specs=(any_space,) * 7,
        scratch_shapes=scratch,
        compiler_params=pltpu.CompilerParams(
            collective_id=0, has_side_effects=True, vmem_limit_bytes=32 * 1024 * 1024
        ),
        name="retention_backward",
    )(*(
        pltpu.with_memory_space_constraint(a, pltpu.HBM)
        for a in (doc_starts, log_decay, out_grad, out_proj, query_rows, key_rows, value_rows)
    ))
    return pl.pallas_call(
        finish,
        out_shape=(result, result, result),
        in_specs=[pl.BlockSpec(memory_space=pltpu.VMEM)] * 6 + [any_space],
        out_specs=(any_space,) * 3,
        scratch_shapes=[
            pltpu.VMEM((tokens, size), F32),
            pltpu.VMEM((tokens, size), F32),
            pltpu.SemaphoreType.DMA((3, 4)),
        ],
        compiler_params=pltpu.CompilerParams(vmem_limit_bytes=16 * 1024 * 1024),
        name="finish",
    )(adjoint, outflow, key_rows, value_rows, k_part, v_part, q_part)


def solution(mesh):
    lines = PLANE
    planes = mesh.shape["ctx"] // (2 * lines)
    return jax.shard_map(
        functools.partial(on_device, planes, lines),
        mesh=mesh,
        in_specs=(
            P("ctx", "head"),
            P("head", None),
            P("ctx", "head"),
            P("ctx", "head"),
            P("ctx", "head"),
            P("head", "ctx"),
            P(),
        ),
        out_specs=(P("ctx", "head"), P("ctx", "head"), P("ctx", "head")),
        check_vma=False,
    )
```

```python
import functools

import jax
import jax.numpy as jnp
from jax import lax
from jax.experimental import pallas as pl
from jax.experimental.pallas import tpu as pltpu
from jax.sharding import PartitionSpec as P

PLANE = 4
CHUNKS = 4
MESH = pl.DeviceIdType.MESH
F32 = jnp.float32
BF16 = jnp.bfloat16


def nn(a, b):
    return lax.dot_general(a, b, (((1,), (0,)), ((), ())), preferred_element_type=F32)


def nt(a, b):
    return lax.dot_general(a, b, (((1,), (1,)), ((), ())), preferred_element_type=F32)


def tn(a, b):
    return lax.dot_general(a, b, (((0,), (0,)), ((), ())), preferred_element_type=F32)


def far_first(n, size):
    half = size // 2
    return half + lax.rem(n + 1, 2) * (n // 2) - lax.rem(n, 2) * ((n + 1) // 2)


def ring_offsets(distance, size):
    return sorted({distance % size, -distance % size} - {0})


def kernel(
    planes, lines,
    doc_in, ld_in, og, w, q, k, v,
    qg, kg, vg, adjoint, outflow, k_out, v_out,
    doc, ld, og_v, w_v, w_t, q_v, k_v, v_v, acc, g_v, wt, sm, fm, dq, inc, outc, qg_v, kg_v, vg_v, oc_v,
    t_send, t_other, tc_send, t_rec, own, core_send, core_rec, ch_send, ch_rec, en_send, en_rec,
    back_send, back_rec, state,
    local_sem, out_sem, y_send, y_rec, t_sem, c_send, c_rec, greet_sem,
):
    tokens, width = q_v.shape
    feats = og_v.shape[2]
    size = width // 2
    chips, height, wide = ch_send.shape[1:]
    chunk = tokens // CHUNKS
    factor = size ** -0.5
    ctx, y = lax.axis_index("ctx"), lax.axis_index("head")
    chip, core = ctx // 2, ctx % 2
    z, x = chip // lines, chip % lines
    first_core = core == 0
    other = chip * 2 + 1 - core
    right, left = (y + 1) % 4, (y + 3) % 4
    owners = (y, left, right, (y + 2) % 4)

    def at_chip(dz, dx):
        return (((z + dz) % planes * lines + (x + dx) % lines) * 2 + core, y)

    near_z, far_z = ring_offsets(1, planes), ring_offsets(2, planes)
    near_x = [at_chip(0, d) for d in ring_offsets(1, lines)]
    near_z, far_z = [at_chip(d, 0) for d in near_z], [at_chip(d, 0) for d in far_z]
    rounds = [near_z + near_x, near_z + far_z, far_z]
    barrier = pltpu.get_barrier_semaphore()
    entry = [(ctx, left), (ctx, right), (other, y)] + near_z + near_x
    for near in entry:
        pl.semaphore_signal(barrier, inc=1, device_id=near, device_id_type=MESH)
    loads = [pltpu.make_async_copy(og, og_v.at[0], local_sem.at[0])]
    for i, (src, dst) in enumerate(((k, k_v), (v, v_v), (q, q_v))):
        loads.append(pltpu.make_async_copy(src, dst, local_sem.at[1 + i]))
    for i in range(4):
        start = pl.multiple_of(owners[i] * feats, 128)
        loads.append(pltpu.make_async_copy(w.at[:, pl.ds(start, feats)], w_v.at[i], local_sem.at[4 + i]))
    small = [pltpu.make_async_copy(ld_in, ld, local_sem.at[8]), pltpu.make_async_copy(doc_in, doc, local_sem.at[9])]
    for load in small + loads:
        load.start()
    pl.semaphore_wait(barrier, len(entry))

    def tell(i):
        for to in rounds[i]:
            pl.semaphore_signal(greet_sem.at[i], inc=1, device_id=to, device_id_type=MESH)

    def hear(i):
        if rounds[i]:
            pl.semaphore_wait(greet_sem.at[i], len(rounds[i]))

    def hop(src_slot, dst_slot, c, to, lane):
        at = pl.ds(c * chunk, chunk)
        return pltpu.make_async_remote_copy(
            src_ref=og_v.at[src_slot, at], dst_ref=og_v.at[dst_slot, at],
            send_sem=y_send.at[lane, c], recv_sem=y_rec.at[dst_slot - 1, c],
            device_id=(ctx, to), device_id_type=MESH,
        )

    to_right = [hop(0, 1, c, right, 0) for c in range(CHUNKS)]
    to_left = [hop(0, 2, c, left, 1) for c in range(CHUNKS)]
    onward = [hop(1, 3, c, right, 2) if c < CHUNKS // 2 else hop(2, 3, c, left, 2) for c in range(CHUNKS)]
    loads[0].wait()
    for c in range(CHUNKS):
        to_right[c].start()
        to_left[CHUNKS - 1 - c].start()
    tell(0)

    offset = ctx * tokens
    lane = lax.broadcasted_iota(jnp.int32, (8, tokens), 1)
    for load in small:
        load.wait()
    docs = [doc[i] for i in range(doc.shape[0])]

    def segment(places):
        total = jnp.zeros(places.shape, jnp.int32)
        for d in docs:
            total = total + (d <= places).astype(jnp.int32)
        return total

    def segment_at(place):
        total = jnp.int32(0)
        for d in docs:
            total = total + (d <= place).astype(jnp.int32)
        return total

    before, last = segment_at(offset - 1), segment_at(offset + tokens - 1)
    seg_row = segment(offset + lane)[0:1]
    row_at = lax.broadcasted_iota(jnp.int32, (tokens, tokens), 0)
    col_at = lax.broadcasted_iota(jnp.int32, (tokens, tokens), 1)
    seg_col = segment(offset + lax.broadcasted_iota(jnp.int32, (tokens, 1), 0))
    in_col = (seg_col == before).astype(F32)
    out_col = (seg_col == last).astype(F32)
    same = (seg_col == seg_row) & (col_at <= row_at)
    cums = []
    for h in range(2):
        cum = jnp.broadcast_to(ld[h : h + 1, :], (8, tokens))
        step = 1
        while step < tokens:
            cum = cum + jnp.where(lane >= step, pltpu.roll(cum, step, 1), 0.0)
            step *= 2
        whole = jnp.sum(jnp.where(lane == tokens - 1, cum, 0.0), axis=1, keepdims=True)
        through = jnp.exp(whole) * jnp.where(before == last, 1.0, 0.0)
        t_send[h] = jnp.broadcast_to(through, (8, t_send.shape[2]))
        cum_row = cum[0:1]
        cum_col = jnp.sum(jnp.where(row_at == col_at, cum_row, 0.0), axis=1, keepdims=True)
        inc[h] = jnp.exp(cum_col) * in_col
        outc[h] = jnp.exp(whole[0:1] - cum_col) * out_col
        cums.append((cum_row, cum_col))

    def to_core(src, dst, send, recv):
        return pltpu.make_async_remote_copy(
            src_ref=src, dst_ref=dst, send_sem=send, recv_sem=recv,
            device_id=(other, y), device_id_type=MESH,
        )

    def apart(d, size):
        return min(d, size - d)

    offsets = [(a, b) for a in range(planes) for b in range(lines) if a or b]
    offsets.sort(key=lambda o: -apart(o[0], planes) - apart(o[1], lines))

    def to_chips(src, dst, send, recv, index):
        for a, b in offsets:
            j = (z + a) % planes * lines + (x + b) % lines
            pltpu.make_async_remote_copy(
                src_ref=src.at[index(j)], dst_ref=dst.at[chip], send_sem=send, recv_sem=recv,
                device_id=(j * 2 + core, y), device_id_type=MESH,
            ).start()

    def arrived(ref, count, sem):
        part = ref.at[pl.ds(0, count)]
        pltpu.make_async_copy(part, part, sem).wait()

    t_copy = to_core(t_send.at[1 - core], t_other, t_sem.at[0], t_sem.at[1])
    t_copy.start()

    def decay(ref):
        return ref[0:1, 0:1]

    def core_copy(direction):
        return to_core(
            core_send.at[direction], core_rec.at[direction], c_send.at[direction, 0], c_rec.at[direction, 0]
        )

    def back_copy(direction):
        return to_core(
            back_send.at[direction], adjoint if direction else back_rec, c_send.at[direction, 3], c_rec.at[direction, 3]
        )

    def first_send(direction):
        core_send[direction] = own[direction, 1 - core].astype(BF16)
        core_copy(direction).start()

    def pieces(ref, direction, whole):
        half = chips // 2 if chips > 1 else 1
        for i in range(2):
            part = whole[:, i * wide : (i + 1) * wide]
            ref[direction, i * half : (i + 1) * half] = part.reshape(half, height, wide)

    def second_send(direction):
        core_copy(direction).wait_recv()
        mine, theirs = own[direction, core], core_rec[direction].astype(F32)
        earlier = first_core if direction == 0 else jnp.logical_not(first_core)
        a = jnp.where(earlier, decay(t_other), 1.0)
        b = jnp.where(earlier, 1.0, decay(t_send.at[core]))
        pieces(ch_send, direction, (a * mine + b * theirs).astype(BF16))
        to_chips(
            ch_send.at[direction], ch_rec.at[direction], c_send.at[direction, 1], c_rec.at[direction, 1],
            lambda j: j,
        )
        ch_rec[direction, chip] = ch_send[direction, chip]

    def third_send(direction):
        arrived(ch_rec.at[direction], chips - 1, c_rec.at[direction, 1])
        run = jnp.zeros((height // 8, 8, wide), F32)
        for i in range(chips) if direction == 0 else reversed(range(chips)):
            en_send[direction, i] = run.reshape(height, wide).astype(BF16)
            here = ch_rec[direction, i].astype(F32).reshape(height // 8, 8, wide)
            run = t_rec[i, :, 0:wide] * run + here
        to_chips(
            en_send.at[direction], en_rec.at[direction], c_send.at[direction, 2], c_rec.at[direction, 2],
            lambda j: j,
        )
        en_rec[direction, chip] = en_send[direction, chip]

    def fourth_send(direction):
        arrived(en_rec.at[direction], chips - 1, c_rec.at[direction, 2])
        half = chips // 2
        parts = [en_rec[direction, i * half : (i + 1) * half].reshape(size, wide) for i in range(2)]
        entering = jnp.concatenate(parts, axis=1).astype(F32)
        earlier = first_core if direction == 0 else jnp.logical_not(first_core)
        a = jnp.where(earlier, decay(t_send.at[core]), 1.0)
        b = jnp.where(earlier, 1.0, 0.0)
        back_send[direction] = (a * entering + b * own[direction, core]).astype(BF16)
        back_copy(direction).start()
        a = jnp.where(earlier, 1.0, decay(t_other))
        return (a * entering + (1.0 - b) * core_rec[direction].astype(F32)).astype(BF16)

    def cols(h):
        return slice(h * size, (h + 1) * size)

    loads[1].wait()
    loads[2].wait()
    for h in range(2):
        decayed = (k_v[:, cols(h)].astype(F32) * outc[h]).astype(BF16)
        own[0, h] = tn(decayed, v_v[:, cols(h)])
    first_send(0)
    hear(0)
    tell(1)

    loads[3].wait()
    q_v[...] = q_v[...] * jnp.asarray(factor, BF16)
    at_lane = lax.broadcasted_iota(jnp.int32, oc_v.shape, 1)
    oc_v[...] = jnp.where(at_lane == 0, outc[0], outc[1])
    for h in range(2):
        dq[h] = (q_v[:, cols(h)].astype(F32) * inc[h]).astype(BF16).T
        cum_row, cum_col = cums[h]
        wt[h] = jnp.exp(jnp.where(same, cum_col - cum_row, -1e30))
        sm[h] = (nt(q_v[:, cols(h)], k_v[:, cols(h)]) * wt[h]).astype(BF16)
    hear(1)
    tell(2)
    loads[4].wait()
    acc[...] = nt(og_v[0], w_v[0])
    for i in range(1, 4):
        loads[4 + i].wait()
        w_t[i - 1] = w_v[i].T
    hear(2)
    t_copy.wait_recv()
    tc_send[...] = t_send[core] * t_other[...]
    to_chips(tc_send, t_rec, t_sem.at[2], t_sem.at[3], lambda j: slice(None))
    t_rec[chip] = tc_send[...]
    second_send(0)

    def add(slot, c):
        at = slice(c * chunk, (c + 1) * chunk)
        acc[at, :] += nn(og_v[slot, at], w_t[slot - 1])

    half = CHUNKS // 2
    for c in range(half):
        to_right[c].wait_recv()
        onward[c].start()
        to_left[CHUNKS - 1 - c].wait_recv()
        onward[CHUNKS - 1 - c].start()
        add(1, c)
        add(2, CHUNKS - 1 - c)
    for c in range(half):
        to_right[half + c].wait_recv()
        add(1, half + c)
        to_left[half - 1 - c].wait_recv()
        add(2, half - 1 - c)

    for c in range(half):
        for at in (c, CHUNKS - 1 - c):
            onward[at].wait_recv()
            span = slice(at * chunk, (at + 1) * chunk)
            g_v[span, :] = (acc[span, :] + nn(og_v[3, span], w_t[2])).astype(BF16)
    for h in (1 - core, core):
        at = pl.ds(pl.multiple_of(h * size, 128), size)
        own[1, h] = nn(dq[h], g_v[:, at])
        if h is not core:
            first_send(1)

    outs = [pltpu.make_async_copy(oc_v, outflow, out_sem.at[3, 0])]
    for i, (src, dst) in enumerate(((k_v, k_out), (v_v, v_out))):
        outs.append(pltpu.make_async_copy(src, dst, out_sem.at[4, i]))
    for copy in outs:
        copy.start()

    def put(src, dst, h, i):
        copy = pltpu.make_async_copy(src.at[:, cols(h)], dst.at[:, cols(h)], out_sem.at[i, h])
        copy.start()
        outs.append(copy)

    second_send(1)
    for h in range(2):
        fm[h] = (nt(g_v[:, cols(h)], v_v[:, cols(h)]) * wt[h]).astype(BF16)
    arrived(t_rec, chips - 1, t_sem.at[3])
    third_send(0)
    for h in range(2):
        kg_v[:, cols(h)] = tn(fm[h], q_v[:, cols(h)])
        vg_v[:, cols(h)] = tn(sm[h], g_v[:, cols(h)])
    third_send(1)
    state[core] = fourth_send(0)
    back_copy(0).wait_recv()
    state[1 - core] = back_rec[...]
    for h in range(2):
        entering = nt(g_v[:, cols(h)], state[h])
        qg_v[:, cols(h)] = factor * (nn(fm[h], k_v[:, cols(h)]) + inc[h] * entering)
        put(qg_v, qg, h, 0)

    for copy in to_right + to_left + onward + [t_copy]:
        copy.wait_send()
    arrived(t_rec, chips - 1, t_sem.at[2])
    for direction in range(2):
        core_copy(direction).wait_send()
        arrived(ch_send.at[direction], chips - 1, c_send.at[direction, 1])
    arrived(en_send.at[0], chips - 1, c_send.at[0, 2])
    back_copy(0).wait_send()

    mine, theirs = pl.ds(pl.multiple_of(core * size, 128), size), pl.ds(pl.multiple_of(size - core * size, 128), size)
    for i, (src, dst) in enumerate(((kg_v, kg), (vg_v, vg))):
        outs.append(pltpu.make_async_copy(src.at[:, theirs], dst.at[:, theirs], out_sem.at[1 + i, 0]))
        outs[-1].start()
    entering = fourth_send(1)
    for i, (src, dst) in enumerate(((kg_v, kg), (vg_v, vg))):
        src[:, mine] += outc[core] * (nn(k_v[:, mine], entering) if i else nt(v_v[:, mine], entering))
        outs.append(pltpu.make_async_copy(src.at[:, mine], dst.at[:, mine], out_sem.at[1 + i, 1]))
        outs[-1].start()
    arrived(en_send.at[1], chips - 1, c_send.at[1, 2])
    for copy in outs:
        copy.wait()
    back_copy(1).wait()


def finish(adjoint, outflow, k, v, k_part, v_part, q_part, qg, kg, vg, k_all, v_all, sem):
    tokens, width = k.shape
    size = width // 2
    step = tokens // 2
    core = lax.axis_index("ctx") % 2
    done, left = pl.ds(pl.multiple_of(core * size, 128), size), pl.ds(pl.multiple_of(size - core * size, 128), size)
    outs = [
        pltpu.make_async_copy(q_part, qg, sem.at[2, 0]),
        pltpu.make_async_copy(k_part.at[:, done], kg.at[:, done], sem.at[2, 1]),
        pltpu.make_async_copy(v_part.at[:, done], vg.at[:, done], sem.at[2, 2]),
    ]
    for copy in outs:
        copy.start()
    for c in range(2):
        at = slice(c * step, (c + 1) * step)
        rows = pl.ds(c * step, step)
        flow = jnp.where(core == 0, outflow[at, 1:2], outflow[at, 0:1])
        for i, (part, whole, out) in enumerate(((k_part, k_all, kg), (v_part, v_all, vg))):
            term = nn(k[at, left], adjoint[...]) if i else nt(v[at, left], adjoint[...])
            whole[at, :] = part[at, left] + flow * term
            copy = pltpu.make_async_copy(whole.at[rows], out.at[rows, left], sem.at[i, c])
            copy.start()
            outs.append(copy)
    for copy in outs:
        copy.wait()


def on_device(planes, lines, out_grad, out_proj, query_rows, key_rows, value_rows, log_decay, doc_starts):
    tokens, width = query_rows.shape
    feats = out_grad.shape[1]
    size = width // 2
    chips = planes * lines
    height, wide = size * 2 // chips, size // 2
    any_space = pl.BlockSpec(memory_space=pl.ANY)
    result = jax.ShapeDtypeStruct((tokens, width), F32)
    adjoint = jax.ShapeDtypeStruct((size, size), BF16)
    outflow = jax.ShapeDtypeStruct((tokens, 128), F32)
    tile = (8, 128)
    scratch = [
        pltpu.SMEM(doc_starts.shape, doc_starts.dtype),
        pltpu.VMEM(log_decay.shape, F32),
        pltpu.VMEM((4, tokens, feats), BF16),
        pltpu.VMEM((4, width, feats), BF16),
        pltpu.VMEM((3, feats, width), BF16),
        pltpu.VMEM((tokens, width), BF16),
        pltpu.VMEM((tokens, width), BF16),
        pltpu.VMEM((tokens, width), BF16),
        pltpu.VMEM((tokens, width), F32),
        pltpu.VMEM((tokens, width), BF16),
        pltpu.VMEM((2, tokens, tokens), F32),
        pltpu.VMEM((2, tokens, tokens), BF16),
        pltpu.VMEM((2, tokens, tokens), BF16),
        pltpu.VMEM((2, size, tokens), BF16),
        pltpu.VMEM((2, tokens, 1), F32),
        pltpu.VMEM((2, tokens, 1), F32),
        pltpu.VMEM((tokens, width), F32),
        pltpu.VMEM((tokens, width), F32),
        pltpu.VMEM((tokens, width), F32),
        pltpu.VMEM((tokens, 128), F32),
        pltpu.VMEM((2,) + tile, F32),
        pltpu.VMEM(tile, F32),
        pltpu.VMEM(tile, F32),
        pltpu.VMEM((chips,) + tile, F32),
        pltpu.VMEM((2, 2, size, size), F32),
        pltpu.VMEM((2, size, size), BF16),
        pltpu.VMEM((2, size, size), BF16),
        pltpu.VMEM((2, chips, height, wide), BF16),
        pltpu.VMEM((2, chips, height, wide), BF16),
        pltpu.VMEM((2, chips, height, wide), BF16),
        pltpu.VMEM((2, chips, height, wide), BF16),
        pltpu.VMEM((2, size, size), BF16),
        pltpu.VMEM((size, size), BF16),
        pltpu.VMEM((2, size, size), BF16),
        pltpu.SemaphoreType.DMA((10,)),
        pltpu.SemaphoreType.DMA((5, 2)),
        pltpu.SemaphoreType.DMA((3, CHUNKS)),
        pltpu.SemaphoreType.DMA((3, CHUNKS)),
        pltpu.SemaphoreType.DMA((4,)),
        pltpu.SemaphoreType.DMA((2, 4)),
        pltpu.SemaphoreType.DMA((2, 4)),
        pltpu.SemaphoreType.REGULAR((3,)),
    ]
    q_part, k_part, v_part, adjoint, outflow, key_rows, value_rows = pl.pallas_call(
        functools.partial(kernel, planes, lines),
        out_shape=tuple(pltpu.VMEM(a.shape, a.dtype) for a in (result, result, result, adjoint, outflow, key_rows, value_rows)),
        in_specs=[any_space] * 7,
        out_specs=(any_space,) * 7,
        scratch_shapes=scratch,
        compiler_params=pltpu.CompilerParams(
            collective_id=0, has_side_effects=True, vmem_limit_bytes=32 * 1024 * 1024
        ),
        name="retention_backward",
    )(*(
        pltpu.with_memory_space_constraint(a, pltpu.HBM)
        for a in (doc_starts, log_decay, out_grad, out_proj, query_rows, key_rows, value_rows)
    ))
    return pl.pallas_call(
        finish,
        out_shape=(result, result, result),
        in_specs=[pl.BlockSpec(memory_space=pltpu.VMEM)] * 6 + [any_space],
        out_specs=(any_space,) * 3,
        scratch_shapes=[
            pltpu.VMEM((tokens, size), F32),
            pltpu.VMEM((tokens, size), F32),
            pltpu.SemaphoreType.DMA((3, 4)),
        ],
        compiler_params=pltpu.CompilerParams(vmem_limit_bytes=16 * 1024 * 1024),
        name="finish",
    )(adjoint, outflow, key_rows, value_rows, k_part, v_part, q_part)


def solution(mesh):
    lines = PLANE
    planes = mesh.shape["ctx"] // (2 * lines)
    return jax.shard_map(
        functools.partial(on_device, planes, lines),
        mesh=mesh,
        in_specs=(
            P("ctx", "head"),
            P("head", None),
            P("ctx", "head"),
            P("ctx", "head"),
            P("ctx", "head"),
            P("head", "ctx"),
            P(),
        ),
        out_specs=(P("ctx", "head"), P("ctx", "head"), P("ctx", "head")),
        check_vma=False,
    )
```

```python
import functools

import jax
import jax.numpy as jnp
from jax import lax
from jax.experimental import pallas as pl
from jax.experimental.pallas import tpu as pltpu
from jax.sharding import PartitionSpec as P

PLANE = 4
CHUNKS = 8
MESH = pl.DeviceIdType.MESH
F32 = jnp.float32
BF16 = jnp.bfloat16


def nn(a, b):
    return lax.dot_general(a, b, (((1,), (0,)), ((), ())), preferred_element_type=F32)


def nt(a, b):
    return lax.dot_general(a, b, (((1,), (1,)), ((), ())), preferred_element_type=F32)


def tn(a, b):
    return lax.dot_general(a, b, (((0,), (0,)), ((), ())), preferred_element_type=F32)


def far_first(n, size):
    half = size // 2
    return half + lax.rem(n + 1, 2) * (n // 2) - lax.rem(n, 2) * ((n + 1) // 2)


def ring_offsets(distance, size):
    return sorted({distance % size, -distance % size} - {0})


def kernel(
    planes, lines,
    doc_in, ld_in, og, w, q, k, v,
    qg, kg, vg, adjoint, outflow, k_out, v_out,
    doc, ld, og_v, w_v, w_t, q_v, k_v, v_v, acc, g_v, wt, sm, fm, dq, inc, outc, qg_v, kg_v, vg_v, oc_v,
    t_send, t_other, tc_send, t_rec, own, core_send, core_rec, ch_send, ch_rec, en_send, en_rec,
    back_send, back_rec, state,
    local_sem, out_sem, y_send, y_rec, t_sem, c_send, c_rec, greet_sem,
):
    tokens, width = q_v.shape
    feats = og_v.shape[2]
    size = width // 2
    chips, height, wide = ch_send.shape[1:]
    chunk = tokens // CHUNKS
    factor = size ** -0.5
    ctx, y = lax.axis_index("ctx"), lax.axis_index("head")
    chip, core = ctx // 2, ctx % 2
    z, x = chip // lines, chip % lines
    first_core = core == 0
    other = chip * 2 + 1 - core
    right, left = (y + 1) % 4, (y + 3) % 4
    owners = (y, left, right, (y + 2) % 4)

    def at_chip(dz, dx):
        return (((z + dz) % planes * lines + (x + dx) % lines) * 2 + core, y)

    near_z, far_z = ring_offsets(1, planes), ring_offsets(2, planes)
    near_x = [at_chip(0, d) for d in ring_offsets(1, lines)]
    near_z, far_z = [at_chip(d, 0) for d in near_z], [at_chip(d, 0) for d in far_z]
    rounds = [near_z + near_x, near_z + far_z, far_z]
    barrier = pltpu.get_barrier_semaphore()
    entry = [(ctx, left), (ctx, right), (other, y)] + near_z + near_x
    for near in entry:
        pl.semaphore_signal(barrier, inc=1, device_id=near, device_id_type=MESH)
    loads = [pltpu.make_async_copy(og, og_v.at[0], local_sem.at[0])]
    for i, (src, dst) in enumerate(((k, k_v), (v, v_v), (q, q_v))):
        loads.append(pltpu.make_async_copy(src, dst, local_sem.at[1 + i]))
    for i in range(4):
        start = pl.multiple_of(owners[i] * feats, 128)
        loads.append(pltpu.make_async_copy(w.at[:, pl.ds(start, feats)], w_v.at[i], local_sem.at[4 + i]))
    small = [pltpu.make_async_copy(ld_in, ld, local_sem.at[8]), pltpu.make_async_copy(doc_in, doc, local_sem.at[9])]
    for load in small + loads:
        load.start()
    pl.semaphore_wait(barrier, len(entry))

    def tell(i):
        for to in rounds[i]:
            pl.semaphore_signal(greet_sem.at[i], inc=1, device_id=to, device_id_type=MESH)

    def hear(i):
        if rounds[i]:
            pl.semaphore_wait(greet_sem.at[i], len(rounds[i]))

    def hop(src_slot, dst_slot, c, to, lane):
        at = pl.ds(c * chunk, chunk)
        return pltpu.make_async_remote_copy(
            src_ref=og_v.at[src_slot, at] if src_slot else og.at[at], dst_ref=og_v.at[dst_slot, at],
            send_sem=y_send.at[lane, c], recv_sem=y_rec.at[dst_slot - 1, c],
            device_id=(ctx, to), device_id_type=MESH,
        )

    to_right = [hop(0, 1, c, right, 0) for c in range(CHUNKS)]
    to_left = [hop(0, 2, c, left, 1) for c in range(CHUNKS)]
    onward = [hop(1, 3, c, right, 2) if c < CHUNKS // 2 else hop(2, 3, c, left, 2) for c in range(CHUNKS)]
    for c in range(CHUNKS):
        to_right[c].start()
        to_left[CHUNKS - 1 - c].start()
    tell(0)

    offset = ctx * tokens
    lane = lax.broadcasted_iota(jnp.int32, (8, tokens), 1)
    for load in small:
        load.wait()
    docs = [doc[i] for i in range(doc.shape[0])]

    def segment(places):
        total = jnp.zeros(places.shape, jnp.int32)
        for d in docs:
            total = total + (d <= places).astype(jnp.int32)
        return total

    def segment_at(place):
        total = jnp.int32(0)
        for d in docs:
            total = total + (d <= place).astype(jnp.int32)
        return total

    before, last = segment_at(offset - 1), segment_at(offset + tokens - 1)
    seg_row = segment(offset + lane)[0:1]
    row_at = lax.broadcasted_iota(jnp.int32, (tokens, tokens), 0)
    col_at = lax.broadcasted_iota(jnp.int32, (tokens, tokens), 1)
    seg_col = segment(offset + lax.broadcasted_iota(jnp.int32, (tokens, 1), 0))
    in_col = (seg_col == before).astype(F32)
    out_col = (seg_col == last).astype(F32)
    same = (seg_col == seg_row) & (col_at <= row_at)
    cums = []
    for h in range(2):
        cum = jnp.broadcast_to(ld[h : h + 1, :], (8, tokens))
        step = 1
        while step < tokens:
            cum = cum + jnp.where(lane >= step, pltpu.roll(cum, step, 1), 0.0)
            step *= 2
        whole = jnp.sum(jnp.where(lane == tokens - 1, cum, 0.0), axis=1, keepdims=True)
        through = jnp.exp(whole) * jnp.where(before == last, 1.0, 0.0)
        t_send[h] = jnp.broadcast_to(through, (8, t_send.shape[2]))
        cum_row = cum[0:1]
        cum_col = jnp.sum(jnp.where(row_at == col_at, cum_row, 0.0), axis=1, keepdims=True)
        inc[h] = jnp.exp(cum_col) * in_col
        outc[h] = jnp.exp(whole[0:1] - cum_col) * out_col
        cums.append((cum_row, cum_col))

    def to_core(src, dst, send, recv):
        return pltpu.make_async_remote_copy(
            src_ref=src, dst_ref=dst, send_sem=send, recv_sem=recv,
            device_id=(other, y), device_id_type=MESH,
        )

    def apart(d, size):
        return min(d, size - d)

    offsets = [(a, b) for a in range(planes) for b in range(lines) if a or b]
    offsets.sort(key=lambda o: -apart(o[0], planes) - apart(o[1], lines))

    def to_chips(src, dst, send, recv, index):
        for a, b in offsets:
            j = (z + a) % planes * lines + (x + b) % lines
            pltpu.make_async_remote_copy(
                src_ref=src.at[index(j)], dst_ref=dst.at[chip], send_sem=send, recv_sem=recv,
                device_id=(j * 2 + core, y), device_id_type=MESH,
            ).start()

    def arrived(ref, count, sem):
        part = ref.at[pl.ds(0, count)]
        pltpu.make_async_copy(part, part, sem).wait()

    t_copy = to_core(t_send.at[1 - core], t_other, t_sem.at[0], t_sem.at[1])
    t_copy.start()

    def decay(ref):
        return ref[0:1, 0:1]

    def core_copy(direction):
        return to_core(
            core_send.at[direction], core_rec.at[direction], c_send.at[direction, 0], c_rec.at[direction, 0]
        )

    def back_copy(direction):
        return to_core(
            back_send.at[direction], adjoint if direction else back_rec, c_send.at[direction, 3], c_rec.at[direction, 3]
        )

    def first_send(direction):
        core_send[direction] = own[direction, 1 - core].astype(BF16)
        core_copy(direction).start()

    def pieces(ref, direction, whole):
        half = chips // 2 if chips > 1 else 1
        for i in range(2):
            part = whole[:, i * wide : (i + 1) * wide]
            ref[direction, i * half : (i + 1) * half] = part.reshape(half, height, wide)

    def second_send(direction):
        core_copy(direction).wait_recv()
        mine, theirs = own[direction, core], core_rec[direction].astype(F32)
        earlier = first_core if direction == 0 else jnp.logical_not(first_core)
        a = jnp.where(earlier, decay(t_other), 1.0)
        b = jnp.where(earlier, 1.0, decay(t_send.at[core]))
        pieces(ch_send, direction, (a * mine + b * theirs).astype(BF16))
        to_chips(
            ch_send.at[direction], ch_rec.at[direction], c_send.at[direction, 1], c_rec.at[direction, 1],
            lambda j: j,
        )
        ch_rec[direction, chip] = ch_send[direction, chip]

    def third_send(direction):
        arrived(ch_rec.at[direction], chips - 1, c_rec.at[direction, 1])
        run = jnp.zeros((height // 8, 8, wide), F32)
        for i in range(chips) if direction == 0 else reversed(range(chips)):
            en_send[direction, i] = run.reshape(height, wide).astype(BF16)
            here = ch_rec[direction, i].astype(F32).reshape(height // 8, 8, wide)
            run = t_rec[i, :, 0:wide] * run + here
        to_chips(
            en_send.at[direction], en_rec.at[direction], c_send.at[direction, 2], c_rec.at[direction, 2],
            lambda j: j,
        )
        en_rec[direction, chip] = en_send[direction, chip]

    def fourth_send(direction):
        arrived(en_rec.at[direction], chips - 1, c_rec.at[direction, 2])
        half = chips // 2
        parts = [en_rec[direction, i * half : (i + 1) * half].reshape(size, wide) for i in range(2)]
        entering = jnp.concatenate(parts, axis=1).astype(F32)
        earlier = first_core if direction == 0 else jnp.logical_not(first_core)
        a = jnp.where(earlier, decay(t_send.at[core]), 1.0)
        b = jnp.where(earlier, 1.0, 0.0)
        back_send[direction] = (a * entering + b * own[direction, core]).astype(BF16)
        back_copy(direction).start()
        a = jnp.where(earlier, 1.0, decay(t_other))
        return (a * entering + (1.0 - b) * core_rec[direction].astype(F32)).astype(BF16)

    def cols(h):
        return slice(h * size, (h + 1) * size)

    loads[1].wait()
    loads[2].wait()
    for h in range(2):
        decayed = (k_v[:, cols(h)].astype(F32) * outc[h]).astype(BF16)
        own[0, h] = tn(decayed, v_v[:, cols(h)])
    first_send(0)
    hear(0)
    tell(1)

    loads[3].wait()
    q_v[...] = q_v[...] * jnp.asarray(factor, BF16)
    at_lane = lax.broadcasted_iota(jnp.int32, oc_v.shape, 1)
    oc_v[...] = jnp.where(at_lane == 0, outc[0], outc[1])
    for h in range(2):
        dq[h] = (q_v[:, cols(h)].astype(F32) * inc[h]).astype(BF16).T
        cum_row, cum_col = cums[h]
        wt[h] = jnp.exp(jnp.where(same, cum_col - cum_row, -1e30))
        sm[h] = (nt(q_v[:, cols(h)], k_v[:, cols(h)]) * wt[h]).astype(BF16)
    hear(1)
    tell(2)
    loads[0].wait()
    loads[4].wait()
    acc[...] = nt(og_v[0], w_v[0])
    for i in range(1, 4):
        loads[4 + i].wait()
        w_t[i - 1] = w_v[i].T
    hear(2)
    t_copy.wait_recv()
    tc_send[...] = t_send[core] * t_other[...]
    to_chips(tc_send, t_rec, t_sem.at[2], t_sem.at[3], lambda j: slice(None))
    t_rec[chip] = tc_send[...]
    second_send(0)

    def add(slot, c):
        at = slice(c * chunk, (c + 1) * chunk)
        acc[at, :] += nn(og_v[slot, at], w_t[slot - 1])

    half = CHUNKS // 2
    for c in range(half):
        to_right[c].wait_recv()
        onward[c].start()
        to_left[CHUNKS - 1 - c].wait_recv()
        onward[CHUNKS - 1 - c].start()
        add(1, c)
        add(2, CHUNKS - 1 - c)
    for c in range(half):
        to_right[half + c].wait_recv()
        add(1, half + c)
        to_left[half - 1 - c].wait_recv()
        add(2, half - 1 - c)

    for c in range(half):
        for at in (c, CHUNKS - 1 - c):
            onward[at].wait_recv()
            span = slice(at * chunk, (at + 1) * chunk)
            g_v[span, :] = (acc[span, :] + nn(og_v[3, span], w_t[2])).astype(BF16)
    for h in (1 - core, core):
        at = pl.ds(pl.multiple_of(h * size, 128), size)
        own[1, h] = nn(dq[h], g_v[:, at])
        if h is not core:
            first_send(1)

    outs = [pltpu.make_async_copy(oc_v, outflow, out_sem.at[3, 0])]
    for i, (src, dst) in enumerate(((k_v, k_out), (v_v, v_out))):
        outs.append(pltpu.make_async_copy(src, dst, out_sem.at[4, i]))
    for copy in outs:
        copy.start()

    def put(src, dst, h, i):
        copy = pltpu.make_async_copy(src.at[:, cols(h)], dst.at[:, cols(h)], out_sem.at[i, h])
        copy.start()
        outs.append(copy)

    second_send(1)
    for h in range(2):
        fm[h] = (nt(g_v[:, cols(h)], v_v[:, cols(h)]) * wt[h]).astype(BF16)
    arrived(t_rec, chips - 1, t_sem.at[3])
    third_send(0)
    for h in range(2):
        kg_v[:, cols(h)] = tn(fm[h], q_v[:, cols(h)])
        vg_v[:, cols(h)] = tn(sm[h], g_v[:, cols(h)])
    third_send(1)
    state[core] = fourth_send(0)
    back_copy(0).wait_recv()
    state[1 - core] = back_rec[...]
    for h in range(2):
        entering = nt(g_v[:, cols(h)], state[h])
        qg_v[:, cols(h)] = factor * (nn(fm[h], k_v[:, cols(h)]) + inc[h] * entering)
        put(qg_v, qg, h, 0)

    for copy in to_right + to_left + onward + [t_copy]:
        copy.wait_send()
    arrived(t_rec, chips - 1, t_sem.at[2])
    for direction in range(2):
        core_copy(direction).wait_send()
        arrived(ch_send.at[direction], chips - 1, c_send.at[direction, 1])
    arrived(en_send.at[0], chips - 1, c_send.at[0, 2])
    back_copy(0).wait_send()

    mine, theirs = pl.ds(pl.multiple_of(core * size, 128), size), pl.ds(pl.multiple_of(size - core * size, 128), size)
    for i, (src, dst) in enumerate(((kg_v, kg), (vg_v, vg))):
        outs.append(pltpu.make_async_copy(src.at[:, theirs], dst.at[:, theirs], out_sem.at[1 + i, 0]))
        outs[-1].start()
    entering = fourth_send(1)
    for i, (src, dst) in enumerate(((kg_v, kg), (vg_v, vg))):
        src[:, mine] += outc[core] * (nn(k_v[:, mine], entering) if i else nt(v_v[:, mine], entering))
        outs.append(pltpu.make_async_copy(src.at[:, mine], dst.at[:, mine], out_sem.at[1 + i, 1]))
        outs[-1].start()
    arrived(en_send.at[1], chips - 1, c_send.at[1, 2])
    for copy in outs:
        copy.wait()
    back_copy(1).wait()


def finish(adjoint, outflow, k, v, k_part, v_part, q_part, qg, kg, vg, k_all, v_all, sem):
    tokens, width = k.shape
    size = width // 2
    step = tokens // 2
    core = lax.axis_index("ctx") % 2
    done, left = pl.ds(pl.multiple_of(core * size, 128), size), pl.ds(pl.multiple_of(size - core * size, 128), size)
    outs = [
        pltpu.make_async_copy(q_part, qg, sem.at[2, 0]),
        pltpu.make_async_copy(k_part.at[:, done], kg.at[:, done], sem.at[2, 1]),
        pltpu.make_async_copy(v_part.at[:, done], vg.at[:, done], sem.at[2, 2]),
    ]
    for copy in outs:
        copy.start()
    for c in range(2):
        at = slice(c * step, (c + 1) * step)
        rows = pl.ds(c * step, step)
        flow = jnp.where(core == 0, outflow[at, 1:2], outflow[at, 0:1])
        for i, (part, whole, out) in enumerate(((k_part, k_all, kg), (v_part, v_all, vg))):
            term = nn(k[at, left], adjoint[...]) if i else nt(v[at, left], adjoint[...])
            whole[at, :] = part[at, left] + flow * term
            copy = pltpu.make_async_copy(whole.at[rows], out.at[rows, left], sem.at[i, c])
            copy.start()
            outs.append(copy)
    for copy in outs:
        copy.wait()


def on_device(planes, lines, out_grad, out_proj, query_rows, key_rows, value_rows, log_decay, doc_starts):
    tokens, width = query_rows.shape
    feats = out_grad.shape[1]
    size = width // 2
    chips = planes * lines
    height, wide = size * 2 // chips, size // 2
    any_space = pl.BlockSpec(memory_space=pl.ANY)
    result = jax.ShapeDtypeStruct((tokens, width), F32)
    adjoint = jax.ShapeDtypeStruct((size, size), BF16)
    outflow = jax.ShapeDtypeStruct((tokens, 128), F32)
    tile = (8, 128)
    scratch = [
        pltpu.SMEM(doc_starts.shape, doc_starts.dtype),
        pltpu.VMEM(log_decay.shape, F32),
        pltpu.VMEM((4, tokens, feats), BF16),
        pltpu.VMEM((4, width, feats), BF16),
        pltpu.VMEM((3, feats, width), BF16),
        pltpu.VMEM((tokens, width), BF16),
        pltpu.VMEM((tokens, width), BF16),
        pltpu.VMEM((tokens, width), BF16),
        pltpu.VMEM((tokens, width), F32),
        pltpu.VMEM((tokens, width), BF16),
        pltpu.VMEM((2, tokens, tokens), F32),
        pltpu.VMEM((2, tokens, tokens), BF16),
        pltpu.VMEM((2, tokens, tokens), BF16),
        pltpu.VMEM((2, size, tokens), BF16),
        pltpu.VMEM((2, tokens, 1), F32),
        pltpu.VMEM((2, tokens, 1), F32),
        pltpu.VMEM((tokens, width), F32),
        pltpu.VMEM((tokens, width), F32),
        pltpu.VMEM((tokens, width), F32),
        pltpu.VMEM((tokens, 128), F32),
        pltpu.VMEM((2,) + tile, F32),
        pltpu.VMEM(tile, F32),
        pltpu.VMEM(tile, F32),
        pltpu.VMEM((chips,) + tile, F32),
        pltpu.VMEM((2, 2, size, size), F32),
        pltpu.VMEM((2, size, size), BF16),
        pltpu.VMEM((2, size, size), BF16),
        pltpu.VMEM((2, chips, height, wide), BF16),
        pltpu.VMEM((2, chips, height, wide), BF16),
        pltpu.VMEM((2, chips, height, wide), BF16),
        pltpu.VMEM((2, chips, height, wide), BF16),
        pltpu.VMEM((2, size, size), BF16),
        pltpu.VMEM((size, size), BF16),
        pltpu.VMEM((2, size, size), BF16),
        pltpu.SemaphoreType.DMA((10,)),
        pltpu.SemaphoreType.DMA((5, 2)),
        pltpu.SemaphoreType.DMA((3, CHUNKS)),
        pltpu.SemaphoreType.DMA((3, CHUNKS)),
        pltpu.SemaphoreType.DMA((4,)),
        pltpu.SemaphoreType.DMA((2, 4)),
        pltpu.SemaphoreType.DMA((2, 4)),
        pltpu.SemaphoreType.REGULAR((3,)),
    ]
    q_part, k_part, v_part, adjoint, outflow, key_rows, value_rows = pl.pallas_call(
        functools.partial(kernel, planes, lines),
        out_shape=tuple(pltpu.VMEM(a.shape, a.dtype) for a in (result, result, result, adjoint, outflow, key_rows, value_rows)),
        in_specs=[any_space] * 7,
        out_specs=(any_space,) * 7,
        scratch_shapes=scratch,
        compiler_params=pltpu.CompilerParams(
            collective_id=0, has_side_effects=True, vmem_limit_bytes=32 * 1024 * 1024
        ),
        name="retention_backward",
    )(*(
        pltpu.with_memory_space_constraint(a, pltpu.HBM)
        for a in (doc_starts, log_decay, out_grad, out_proj, query_rows, key_rows, value_rows)
    ))
    return pl.pallas_call(
        finish,
        out_shape=(result, result, result),
        in_specs=[pl.BlockSpec(memory_space=pltpu.VMEM)] * 6 + [any_space],
        out_specs=(any_space,) * 3,
        scratch_shapes=[
            pltpu.VMEM((tokens, size), F32),
            pltpu.VMEM((tokens, size), F32),
            pltpu.SemaphoreType.DMA((3, 4)),
        ],
        compiler_params=pltpu.CompilerParams(vmem_limit_bytes=16 * 1024 * 1024),
        name="finish",
    )(adjoint, outflow, key_rows, value_rows, k_part, v_part, q_part)


def solution(mesh):
    lines = PLANE
    planes = mesh.shape["ctx"] // (2 * lines)
    return jax.shard_map(
        functools.partial(on_device, planes, lines),
        mesh=mesh,
        in_specs=(
            P("ctx", "head"),
            P("head", None),
            P("ctx", "head"),
            P("ctx", "head"),
            P("ctx", "head"),
            P("head", "ctx"),
            P(),
        ),
        out_specs=(P("ctx", "head"), P("ctx", "head"), P("ctx", "head")),
        check_vma=False,
    )
```
